512 devices in a mesh: wide: 64 (over z_lo, y, core), narrow: 8 (over z_hi, x).
Axes of the slice: x: 4, y: 4, z: 16 (z_hi: 2, z_lo: 8; z = z_hi * 8 + z_lo), core: 2. Of those that a mesh axis runs over, the one named last changes fastest.
Arguments:
- prior: float32 [384, 32, 384], P('wide', 'narrow'), may hold values from -6 to 6
- coil_maps: bfloat16 [384, 196608], P('wide', 'narrow'), may hold values from -1.5 to 1.5
- kspace: bfloat16 [2, 384, 196608], P(None, None, ('narrow', 'wide')), may hold values from -6 to 6
- band_start: int32 [2, 12288], P(None, ('narrow', 'wide')), may hold values from -12 to 12
- band_frac: float32 [2, 384, 12288], P(None, None, ('narrow', 'wide')), may hold values from 0 to 1
- shot_mask: int32 [2, 6, 32], P(None, None, 'narrow'), may hold values 0 or 1
Outputs:
- solution: float32 [384, 12288], P(None, ('narrow', 'wide'))
- denoised: float32 [384, 32, 384], P('wide', 'narrow')
The draws below stay inside these ranges and needn't reach their ends.
All inputs are finite; a program needn't handle non-finite values. No bound on the sum of `shot_mask` on one device may be relied on, other than what follows from the above.
Results may differ from the reference program's by a relative error of at most 0.0033.
Values may be sent and summed in bfloat16 or wider, within the bound.
A program may use at most 64 MiB of HBM per device.

```python
import math
import jax
import jax.numpy as jnp
from jax import lax

NY = 384
NX = 384
COILS = 16
BLIPS = 2
SHOTS = 6
TAPS = 8
CG_ITERS = 2
DIFF_STEPS = 3
NZ = 32
COLUMNS = 12288


def draw_kspace(key, part):
    key = jax.random.fold_in(key, 11)
    full_shape = (BLIPS, NY, NZ * NX * COILS)
    column_pos = (jnp.arange(NZ * NX * COILS, dtype=jnp.int32) // COILS).astype(jnp.float32)
    scale_row = 0.5 + column_pos / (NZ * NX)
    base_values = jnp.clip(jax.random.normal(key, full_shape, jnp.float32), -4.0, 4.0)
    return (base_values * scale_row[None, None, :]).astype(jnp.bfloat16)


def set_ends(values, stream_key, low, top_value):
    index_at = [jax.random.randint(jax.random.fold_in(stream_key, axis), (), 0, length) for axis, length in enumerate(values.shape)]
    longest = values.shape.index(max(values.shape))
    neighbour = index_at[:longest] + [(index_at[longest] + 1) % values.shape[longest]] + index_at[longest + 1:]
    return values.at[tuple(index_at)].set(low).at[tuple(neighbour)].set(top_value)


def block_levels(own_key, dims, cuts, least, high):
    def one(position, shards_of):
        heights = jax.random.uniform(jax.random.fold_in(jax.random.fold_in(own_key, 6), position), (shards_of,), jnp.float32, least / len(cuts), high / len(cuts))
        return jnp.repeat(jnp.exp(heights), dims[position] // shards_of).reshape((-1,) + (1,) * (len(dims) - position - 1))

    gain = one(*cuts[0])
    for cut in cuts[1:]:
        gain = gain * one(*cut)
    return gain


def bell_draw(rng, shape, deviation, reach, shards=(), held_as=jnp.bfloat16):
    values = deviation * jax.random.normal(rng, shape, jnp.float32)
    if shards:
        values = values * block_levels(rng, shape, shards, -0.22, 0.18)
    return jnp.clip(values, -reach, reach).astype(held_as)


def setup_inputs(seed: int = 0) -> dict:
    key_list = jax.random.split(jax.random.key(seed), 7)
    return {
        "prior": bell_draw(key_list[0], (NY, NZ, NX), 1.0, 6.0, ((0, 64), (1, 8)), jnp.float32),
        "coil_maps": bell_draw(key_list[1], (NY, COLUMNS * COILS), 0.25, 1.5, ((0, 64), (1, 8))),
        "kspace": draw_kspace(jax.random.fold_in(key_list[6], 71), 0),
        "band_start": set_ends(jax.random.randint(key_list[3], (BLIPS, COLUMNS), -12, 13), jax.random.fold_in(key_list[3], 1), -12, 12).astype(jnp.int32),
        "band_frac": jnp.clip(1.0 * jax.random.uniform(key_list[4], (BLIPS, NY, COLUMNS), jnp.float32) ** block_levels(key_list[4], (BLIPS, NY, COLUMNS), ((2, 512),), -0.2, 0.2), 0.0, 1.0),
        "shot_mask": set_ends((jax.random.randint(key_list[5], (BLIPS, SHOTS, NZ), 0, 6) < 5).astype(jnp.int32), jax.random.fold_in(key_list[5], 1), 0, 1),
    }


penalty = 0.5
time_step = 0.18
edge_scale = 1.0
low_offset = -15
band_span = 32
axis_weights = (1.0, 0.5, 1.0)

def cosine_tables(length):
    freq_pos = jnp.arange(length, dtype=jnp.float32)[:, None]
    cell_pos = jnp.arange(length, dtype=jnp.float32)[None, :]
    entries = jnp.cos(math.pi * (cell_pos + 0.5) * freq_pos / length) * math.sqrt(2.0 / length)
    entries = entries * jnp.where(freq_pos == 0.0, math.sqrt(0.5), 1.0)
    forward = entries.astype(jnp.bfloat16)
    return (forward, jnp.transpose(forward))

def band_coefficients(band_start, band_frac):
    tap_pos = jnp.arange(TAPS, dtype=jnp.float32)[:, None, None, None] - 3.0
    spacing = tap_pos - band_frac[None]
    weights = jnp.sinc(spacing) * jnp.sinc(spacing / 4.0)
    offsets = jnp.arange(band_span, dtype=jnp.int32) + low_offset
    tap_index = offsets[:, None, None] - band_start[None] + 3
    band_coeff = jnp.zeros((band_span,) + band_frac.shape, jnp.float32)
    for tap_no in range(TAPS):
        hit = (tap_index == tap_no)[:, :, None, :]
        band_coeff = band_coeff + jnp.where(hit, weights[tap_no][None], 0.0)
    return band_coeff

def band_apply(band_coeff, values):
    length = values.shape[0]
    padded = jnp.pad(values, ((-low_offset, band_span - 1 + low_offset), (0, 0)))
    summed = jnp.zeros_like(values)
    for offset_no in range(band_span):
        summed = summed + band_coeff[offset_no] * padded[offset_no:offset_no + length]
    return summed

def band_adjoint(band_coeff, values):
    length = values.shape[0]
    summed = jnp.zeros((length + band_span - 1, values.shape[1]), values.dtype)
    for offset_no in range(band_span):
        summed = summed + jnp.pad(band_coeff[offset_no] * values, ((offset_no, band_span - 1 - offset_no), (0, 0)))
    return summed[-low_offset:-low_offset + length]

def shot_rows(mask_cols, length):
    row_pick = ((jnp.arange(length, dtype=jnp.int32) % SHOTS)[:, None] == jnp.arange(SHOTS, dtype=jnp.int32)[None, :]).astype(jnp.float32)
    return jnp.einsum('ys,psc->pyc', row_pick, mask_cols)

def coil_return(kept_spec, coil_maps, cosine_back, band_coeff):
    length, col_count, coils_here = coil_maps.shape
    returned = jnp.dot(cosine_back, kept_spec, preferred_element_type=jnp.float32).reshape(length, col_count, coils_here)
    combined = lax.optimization_barrier(jnp.sum(returned * coil_maps, axis=2))
    return band_adjoint(band_coeff, combined)

def normal_product(iterate, coil_maps, band_coeff, sampled, cosine_fwd, cosine_back):
    length, col_count, coils_here = coil_maps.shape
    summed = penalty * iterate
    for blip_no in range(BLIPS):
        shifted = band_apply(band_coeff[:, blip_no], iterate)
        coil_images = (coil_maps * shifted[:, :, None]).astype(jnp.bfloat16)
        spectra = jnp.dot(cosine_fwd, coil_images.reshape(length, -1), preferred_element_type=jnp.float32)
        kept_spec = (spectra.reshape(length, col_count, coils_here) * sampled[blip_no][:, :, None]).astype(jnp.bfloat16)
        summed = summed + coil_return(kept_spec.reshape(length, -1), coil_maps, cosine_back, band_coeff[:, blip_no])
    return summed

def data_side(kspace, coil_maps, band_coeff, sampled, cosine_back):
    length, col_count, coils_here = coil_maps.shape
    summed = jnp.zeros((length, col_count), jnp.float32)
    for blip_no in range(BLIPS):
        kept_spec = kspace[blip_no].reshape(length, col_count, coils_here) * sampled[blip_no][:, :, None].astype(jnp.bfloat16)
        summed = summed + coil_return(kept_spec.reshape(length, -1), coil_maps, cosine_back, band_coeff[:, blip_no])
    return summed

def edge_flux(jump_size):
    scaled = jump_size / edge_scale
    return jump_size / (1.0 + scaled * scaled)

def diffuse_once(padded):
    middle = padded[1:-1, 1:-1, 1:-1]
    neighbours = ((padded[2:, 1:-1, 1:-1], padded[:-2, 1:-1, 1:-1]), (padded[1:-1, 2:, 1:-1], padded[1:-1, :-2, 1:-1]), (padded[1:-1, 1:-1, 2:], padded[1:-1, 1:-1, :-2]))
    change = jnp.zeros_like(middle)
    for weight_axis, pair_cells in zip(axis_weights, neighbours):
        change = change + weight_axis * (edge_flux(pair_cells[0] - middle) - edge_flux(middle - pair_cells[1]))
    return middle + time_step * change

def reference(prior, coil_maps, kspace, band_start, band_frac, shot_mask):
    cosine_fwd, cosine_back = cosine_tables(NY)
    maps_slices = coil_maps.reshape(NY, NZ, NX, COILS).transpose(1, 0, 2, 3)
    data_slices = kspace.reshape(BLIPS, NY, NZ, NX * COILS).transpose(2, 0, 1, 3)
    start_slices = band_start.reshape(BLIPS, NZ, NX).transpose(1, 0, 2)
    frac_slices = band_frac.reshape(BLIPS, NY, NZ, NX).transpose(2, 0, 1, 3)
    mask_slices = shot_mask.transpose(2, 0, 1).astype(jnp.float32)
    prior_cols = prior.transpose(1, 0, 2)
    bundle = (maps_slices, start_slices, frac_slices, mask_slices)

    def slice_setup(members):
        maps_one, start_one, frac_one, mask_one = members
        band_coeff = band_coefficients(start_one, frac_one)
        sampled = shot_rows(jnp.broadcast_to(mask_one[:, :, None], (BLIPS, SHOTS, NX)), NY)
        return (maps_one, band_coeff, sampled)

    def right_one(members):
        maps_one, band_coeff, sampled = slice_setup(members[:4])
        return data_side(members[4], maps_one, band_coeff, sampled, cosine_back)

    def normal_one(members):
        maps_one, band_coeff, sampled = slice_setup(members[:4])
        return normal_product(members[4], maps_one, band_coeff, sampled, cosine_fwd, cosine_back)

    def normal_apply(iterate):
        return lax.map(normal_one, bundle + (iterate,))
    rhs_cols = lax.map(right_one, bundle + (data_slices,)) + penalty * prior_cols
    iterate = prior_cols
    residue = rhs_cols - normal_apply(iterate)
    direction = residue
    norm_now = jnp.sum(residue * residue)
    for step_index in range(CG_ITERS):
        mapped = normal_apply(direction)
        step_len = norm_now / jnp.sum(direction * mapped)
        iterate = iterate + step_len * direction
        if step_index + 1 < CG_ITERS:
            residue = residue - step_len * mapped
            norm_next = jnp.sum(residue * residue)
            direction = residue + norm_next / norm_now * direction
            norm_now = norm_next
    solution = iterate.transpose(1, 0, 2).reshape(NY, NZ * NX)
    bricks = iterate.transpose(1, 0, 2)
    for step_index in range(DIFF_STEPS):
        bricks = diffuse_once(jnp.pad(bricks, 1))
    return (solution, bricks)
```

```python
import functools
import math

import jax
import jax.numpy as jnp
import numpy as np
from jax import lax
from jax.experimental import pallas as pl
from jax.experimental.pallas import tpu as pltpu
from jax.sharding import PartitionSpec as P

SHOTS = 6
TAPS = 8
DIFF_STEPS = 3
COILS = 16
WIDE = 64
NARROW = 8
LINES = 384
COLS = 24
ROWS = 6
SLICES = 4
READOUT = 384
SPAN = 512
PIECES = 3
BAND_BITS = 5

penalty = 0.5
time_step = 0.18
axis_weights = (1.0, 0.5, 1.0)

F32 = jnp.float32
BF16 = jnp.bfloat16
MESH = pl.DeviceIdType.MESH


def cosine_table():
    freq = np.arange(LINES, dtype=np.float32)[:, None]
    cell = np.arange(LINES, dtype=np.float32)[None, :]
    angle = np.float32(math.pi) * (cell + np.float32(0.5)) * freq / np.float32(LINES)
    entries = np.cos(angle).astype(np.float32) * np.float32(math.sqrt(2.0 / LINES))
    entries = entries * np.where(freq == 0.0, np.float32(math.sqrt(0.5)), np.float32(1.0))
    return entries.astype(np.float32)


def place_tables():
    place = np.zeros((WIDE * 8, LINES + 128), np.float32)
    for w in range(WIDE):
        for i in range(ROWS):
            place[8 * w + i, ROWS * w + i] = 1.0
        for g in range(2):
            place[8 * w + 6 + g, LINES + g * 64 + w] = 1.0
    order = np.zeros((3 * 128, LINES), np.float32)
    for t in range(3):
        for g in range(2):
            for w in range(WIDE):
                order[t * 128 + g * 64 + w, ROWS * w + 3 * g + t] = 1.0
    return place, order


def lane_iota(rows, lanes):
    return lax.broadcasted_iota(jnp.int32, (rows, lanes), 1)


def gather_body(prior_ref, maps_ref, out_ref, send_buf, own_sem, send_sem, recv_sem):
    me = lax.axis_index("wide")
    barrier = pltpu.get_barrier_semaphore()

    @pl.loop(1, WIDE)
    def _(k):
        pl.semaphore_signal(barrier, inc=1, device_id={"wide": lax.rem(me + k, WIDE)}, device_id_type=MESH)

    lane = lane_iota(8, 128)
    stacked = [jnp.concatenate([prior_ref[t], prior_ref[3 + t]], axis=0) for t in range(3)]
    for q in range(16):
        packed = jnp.zeros((8, 128), F32)
        for t in range(3):
            turned = pltpu.roll(stacked[t], (24 * t - 24 * q) % READOUT, 1)[:, :128]
            packed = jnp.where((lane >= 24 * t) & (lane < 24 * t + 24), turned, packed)
        high = packed.astype(BF16).astype(F32)
        rest = packed - high
        middle = rest.astype(BF16).astype(F32)
        low = rest - middle
        packed = jnp.concatenate([high, middle, low], axis=1)
        for s in range(SLICES):
            d = 16 * s + q
            block = maps_ref[:, d * 384 : (d + 1) * 384].astype(F32)
            message = jnp.concatenate([block, packed[s : s + 1], packed[4 + s : 5 + s]], axis=0)
            send_buf[d] = message.astype(BF16)

    pl.semaphore_wait(barrier, WIDE - 1)

    @pl.loop(1, WIDE)
    def _(k):
        to = lax.rem(me + k, WIDE)
        pltpu.make_async_remote_copy(
            src_ref=send_buf.at[to],
            dst_ref=out_ref.at[me],
            send_sem=send_sem,
            recv_sem=recv_sem,
            device_id={"wide": to},
            device_id_type=MESH,
        ).start()

    own = pltpu.make_async_copy(send_buf.at[me], out_ref.at[me], own_sem)
    own.start()
    own.wait()
    others = pl.ds(0, WIDE - 1)
    pltpu.make_async_copy(send_buf.at[others], send_buf.at[others], send_sem).wait()
    pltpu.make_async_copy(out_ref.at[others], out_ref.at[others], recv_sem).wait()


def gather_columns(prior, coil_maps):
    vmem = pl.BlockSpec(memory_space=pltpu.VMEM)
    return pl.pallas_call(
        gather_body,
        out_shape=jax.ShapeDtypeStruct((WIDE, 8, LINES), BF16),
        in_specs=[vmem, vmem],
        out_specs=vmem,
        scratch_shapes=[
            pltpu.VMEM((WIDE, 8, LINES), BF16),
            pltpu.SemaphoreType.DMA,
            pltpu.SemaphoreType.DMA,
            pltpu.SemaphoreType.DMA,
        ],
        compiler_params=pltpu.CompilerParams(collective_id=0, has_side_effects=True, vmem_limit_bytes=24 << 20),
        name="gather_columns",
    )(prior, coil_maps)


def poly_sin(x):
    x2 = x * x
    return x * (1.0 + x2 * (-1.0 / 6 + x2 * (1.0 / 120 + x2 * (-1.0 / 5040 + x2 * (1.0 / 362880)))))


def poly_cos(x):
    x2 = x * x
    return 1.0 + x2 * (-0.5 + x2 * (1.0 / 24 + x2 * (-1.0 / 720 + x2 * (1.0 / 40320 - x2 * (1.0 / 3628800)))))


def tap_weights(frac):
    near = jnp.minimum(frac, 1.0 - frac) * (math.pi / 2)
    full = 2.0 * poly_sin(near) * poly_cos(near)
    phi = frac * (math.pi / 4)
    sin_a, cos_a = poly_sin(phi), poly_cos(phi)
    rest = (1.0 - frac) * (math.pi / 4)
    sin_b, cos_b = poly_sin(rest), poly_cos(rest)
    quarter = {-3: -sin_b, -2: -cos_a, -1: -cos_b, 0: -sin_a, 1: sin_b, 2: cos_a, 3: cos_b, 4: sin_a}
    weights = []
    for k in range(TAPS):
        n = k - 3
        t = n - frac
        sign = 1.0 if n % 2 else -1.0
        if n in (0, 1):
            small = jnp.abs(t) < 1e-5
            inverse = 1.0 / jnp.where(small, 1.0, t)
            product = (full * inverse) * (quarter[n] * inverse) * (sign * 4.0 / math.pi**2)
            weights.append(jnp.where(small, 1.0, product))
        else:
            inverse = 1.0 / t
            weights.append((full * inverse) * (quarter[n] * inverse) * (sign * 4.0 / math.pi**2))
    return weights


def wide_lines(values):
    return jnp.concatenate([values, jnp.zeros((values.shape[0], SPAN - LINES), F32)], axis=1)


def left(values, count):
    return pltpu.roll(values, (SPAN - count) % SPAN, 1) if count % SPAN else values


def split3(values):
    high = values.astype(BF16)
    rest = values - high.astype(F32)
    middle = rest.astype(BF16)
    low = (rest - middle.astype(F32)).astype(BF16)
    return high, middle, low


def dot(a, b):
    return jnp.dot(a, b, preferred_element_type=F32)


def dot_first(a, b):
    return lax.dot_general(a, b, (((0,), (0,)), ((), ())), preferred_element_type=F32)


def solve_body(
    got_ref, kspace_ref, start_ref, frac_ref, mask_ref, table_ref, turned_ref, place_ref, order_ref,
    fields_ref, prior_ref, sums_ref, maps3_ref, weight_ref, kept_ref,
):
    my_slice = lax.axis_index("wide") // 16
    both = 2 * COLS

    starts = []
    diagonal = lax.broadcasted_iota(jnp.int32, (COLS, COLS), 0) == lax.broadcasted_iota(jnp.int32, (COLS, COLS), 1)
    for p in range(2):
        row = jnp.broadcast_to(start_ref[p : p + 1, :].astype(F32), (COLS, COLS))
        starts.append(jnp.sum(jnp.where(diagonal, row, 0.0), axis=1, keepdims=True))
    ahead = jnp.concatenate(starts, axis=0).astype(jnp.int32) + 12
    bits = [jnp.broadcast_to((ahead >> bit) & 1, (both, SPAN)) == 1 for bit in range(BAND_BITS)]

    frac = jnp.concatenate([frac_ref[0], frac_ref[1]], axis=0)
    for k, weight in enumerate(tap_weights(frac)):
        weight_ref[k] = weight

    lane = lane_iota(1, LINES)
    shot = lax.rem(lane, SHOTS)
    masks = []
    for p in range(2):
        row = jnp.zeros((1, LINES), F32)
        for h in range(SHOTS):
            row = jnp.where(shot == h, mask_ref[p, my_slice, h].astype(F32), row)
        masks.append(row)
    turned = turned_ref[...]
    forward = [(turned.astype(F32) * masks[p]).astype(BF16) for p in range(2)]

    got = got_ref[...].reshape(WIDE * 8, LINES)
    laid = dot_first(got, place_ref[...])
    maps3_ref[...] = laid[:, :LINES].reshape(COLS, COILS, LINES)
    pieces = []
    for m in range(PIECES):
        parts = [laid[m * 128 + 24 * t : m * 128 + 24 * t + 24, LINES:] for t in range(3)]
        pieces.append(jnp.concatenate(parts, axis=1))
    ordered = dot(jnp.concatenate(pieces, axis=0).astype(BF16), order_ref[...])
    prior = ordered[:COLS] + ordered[COLS : 2 * COLS] + ordered[2 * COLS :]
    prior_ref[...] = prior

    def band_apply(field):
        value = wide_lines(jnp.concatenate([field, field], axis=0))
        value = left(value, -15)
        for bit in range(BAND_BITS):
            value = jnp.where(bits[bit], left(value, 1 << bit), value)
        total = jnp.zeros((both, LINES), F32)
        for k in range(TAPS):
            total = total + weight_ref[k] * left(value, k)[:, :LINES]
        return total

    def band_adjoint(values):
        total = jnp.zeros((both, SPAN), F32)
        for k in range(TAPS):
            total = total + left(wide_lines(weight_ref[k] * values), -k)
        for bit in range(BAND_BITS):
            total = jnp.where(bits[bit], left(total, -(1 << bit)), total)
        total = left(total, 15)
        return (total[:COLS] + total[COLS:])[:, :LINES]

    def through(field):
        moved = band_apply(field)
        back = []
        for p in range(2):
            image = maps3_ref[...] * moved[p * COLS : (p + 1) * COLS][:, None, :]
            image = image.reshape(COLS * COILS, LINES).astype(BF16)
            kept = dot(image, forward[p]).astype(BF16)
            back.append(dot(kept, table_ref[...]))
        return back

    def combine(back):
        return jnp.sum(back.reshape(COLS, COILS, LINES) * maps3_ref[...], axis=1)

    for p in range(2):
        masked = kspace_ref[p]
        kept_ref[p] = lax.dot_general(
            masked, forward[p], (((0,), (1,)), ((), ())), preferred_element_type=F32
        )
    back = through(prior)
    residue = band_adjoint(jnp.concatenate([combine(kept_ref[p] - back[p]) for p in range(2)], axis=0))
    back = through(residue)
    first = band_adjoint(jnp.concatenate([combine(back[p]) for p in range(2)], axis=0))
    back = through(first)
    second = band_adjoint(jnp.concatenate([combine(back[p]) for p in range(2)], axis=0))
    fields_ref[...] = jnp.concatenate([residue, first], axis=0)

    def total(values):
        folded = jnp.sum(values.reshape(3, 8, LINES), axis=0)
        folded = folded[:, :128] + folded[:, 128:256] + folded[:, 256:]
        return jnp.sum(folded, axis=0, keepdims=True)

    sums = [total(residue * residue), total(residue * first), total(first * first), total(first * second)]
    sums_ref[...] = jnp.concatenate(sums + [jnp.zeros((4, 128), F32)], axis=0)


def solve_columns(got, kspace, band_start, frac, mask):
    vmem = pl.BlockSpec(memory_space=pltpu.VMEM)
    table = cosine_table()
    place, order = place_tables()
    return pl.pallas_call(
        solve_body,
        out_shape=(
            jax.ShapeDtypeStruct((2 * COLS, LINES), F32),
            jax.ShapeDtypeStruct((COLS, LINES), F32),
            jax.ShapeDtypeStruct((8, 128), F32),
        ),
        in_specs=[vmem] * 4 + [pl.BlockSpec(memory_space=pltpu.SMEM)] + [vmem] * 4,
        out_specs=(vmem, vmem, vmem),
        scratch_shapes=[
            pltpu.VMEM((COLS, COILS, LINES), F32),
            pltpu.VMEM((TAPS, 2 * COLS, LINES), F32),
            pltpu.VMEM((2, COLS * COILS, LINES), F32),
        ],
        compiler_params=pltpu.CompilerParams(vmem_limit_bytes=48 << 20),
        name="solve_columns",
    )(
        got, kspace, band_start, frac, mask,
        jnp.asarray(table, BF16), jnp.asarray(table.T, BF16), jnp.asarray(place, BF16), jnp.asarray(order, BF16),
    )


def step_scalars(rr, ra, aa, ab):
    alpha = rr / (penalty * rr + ra)
    rho = ra / rr
    qq = jnp.maximum(aa - rho * ra, 0.0)
    qaq = ab - 2.0 * rho * aa + rho * rho * ra
    next_rr = alpha * alpha * qq
    beta = next_rr / rr
    direction_sq = next_rr + beta * beta * rr
    direction_a = alpha * alpha * qaq - 2.0 * beta * alpha * qq + beta * beta * ra
    image = jnp.maximum(penalty * direction_sq + direction_a, penalty * direction_sq)
    second = jnp.where(image > 0.0, next_rr / jnp.where(image > 0.0, image, 1.0), 0.0)
    return alpha + second * (alpha * rho + beta), -second * alpha


def padded_2(cells, sides, width):
    for axis, dim in sides:
        count = lax.axis_size(axis)
        ends = count - 1
        head = lax.slice_in_dim(cells, 0, width, axis=dim)
        tail = lax.slice_in_dim(cells, cells.shape[dim] - width, cells.shape[dim], axis=dim)
        cells = jnp.concatenate(
            [
                lax.ppermute(tail, axis, [(i, (i + 1) % count) for i in range(ends)]),
                cells,
                lax.ppermute(head, axis, [((i + 1) % count, i) for i in range(ends)]),
            ],
            axis=dim,
        )
    return cells


def edge_flux(jump):
    return jump / (1.0 + jump * jump)


def diffuse_once(padded):
    middle = padded[1:-1, 1:-1, 1:-1]
    neighbours = (
        (padded[2:, 1:-1, 1:-1], padded[:-2, 1:-1, 1:-1]),
        (padded[1:-1, 2:, 1:-1], padded[1:-1, :-2, 1:-1]),
        (padded[1:-1, 1:-1, 2:], padded[1:-1, 1:-1, :-2]),
    )
    change = jnp.zeros_like(middle)
    for weight_axis, pair_cells in zip(axis_weights, neighbours):
        change = change + weight_axis * (edge_flux(pair_cells[0] - middle) - edge_flux(middle - pair_cells[1]))
    return middle + time_step * change


def per_device(prior, coil_maps, kspace, band_start, band_frac, shot_mask):
    got = gather_columns(prior, coil_maps)
    fields, prior_cols, sums = solve_columns(
        got, kspace, band_start, jnp.transpose(band_frac, (0, 2, 1)), jnp.transpose(shot_mask, (0, 2, 1))
    )
    sums = lax.psum(jnp.sum(sums, axis=1), ("wide", "narrow"))
    c0, c1 = step_scalars(sums[0], sums[1], sums[2], sums[3])
    iterate = jnp.transpose(prior_cols + c0 * fields[:COLS] + c1 * fields[COLS:])
    bricks = lax.all_to_all(iterate, "wide", split_axis=0, concat_axis=1, tiled=True).reshape(ROWS, SLICES, READOUT)
    for _ in range(DIFF_STEPS):
        padded = padded_2(bricks, (("wide", 0), ("narrow", 1)), 1)
        bricks = diffuse_once(jnp.pad(padded, ((0, 0), (0, 0), (1, 1))))
    return iterate, bricks


def solution(mesh):
    in_specs = (
        P("wide", "narrow", None),
        P("wide", "narrow"),
        P(None, None, ("narrow", "wide")),
        P(None, ("narrow", "wide")),
        P(None, None, ("narrow", "wide")),
        P(None, None, "narrow"),
    )
    out_specs = (P(None, ("narrow", "wide")), P("wide", "narrow", None))
    return jax.shard_map(per_device, mesh=mesh, in_specs=in_specs, out_specs=out_specs, check_vma=False)
```

```python
import functools
import math

import jax
import jax.numpy as jnp
import numpy as np
from jax import lax
from jax.experimental import pallas as pl
from jax.experimental.pallas import tpu as pltpu
from jax.sharding import PartitionSpec as P

SHOTS = 6
TAPS = 8
DIFF_STEPS = 3
COILS = 16
WIDE = 64
NARROW = 8
LINES = 384
COLS = 24
ROWS = 6
SLICES = 4
READOUT = 384
SPAN = 512
PIECES = 3
EDGE = DIFF_STEPS
PLACES = ROWS + 2 * EDGE
DENSE = 5
HALO = 24
BAND_BITS = 5

penalty = 0.5
time_step = 0.18
axis_weights = (1.0, 0.5, 1.0)

F32 = jnp.float32
BF16 = jnp.bfloat16
MESH = pl.DeviceIdType.MESH


def cosine_table():
    freq = np.arange(LINES, dtype=np.float32)[:, None]
    cell = np.arange(LINES, dtype=np.float32)[None, :]
    angle = np.float32(math.pi) * (cell + np.float32(0.5)) * freq / np.float32(LINES)
    entries = np.cos(angle).astype(np.float32) * np.float32(math.sqrt(2.0 / LINES))
    entries = entries * np.where(freq == 0.0, np.float32(math.sqrt(0.5)), np.float32(1.0))
    return entries.astype(np.float32)


def place_tables():
    place = np.zeros((WIDE * 8, LINES + 128), np.float32)
    for w in range(WIDE):
        for i in range(ROWS):
            place[8 * w + i, ROWS * w + i] = 1.0
        for g in range(2):
            place[8 * w + 6 + g, LINES + g * 64 + w] = 1.0
    order = np.zeros((3 * 128, LINES), np.float32)
    for t in range(3):
        for g in range(2):
            for w in range(WIDE):
                order[t * 128 + g * 64 + w, ROWS * w + 3 * g + t] = 1.0
    return place, order


def return_tables():
    spread = np.zeros((PLACES * WIDE, LINES), np.float32)
    for i in range(PLACES):
        for w in range(WIDE):
            line = ROWS * w - EDGE + i
            if 0 <= line < LINES:
                spread[i * WIDE + w, line] = 1.0
    rep = np.zeros((128, 2 * READOUT), np.float32)
    for i in range(2):
        for x in range(READOUT):
            rep[48 * i + x % COLS, i * READOUT + x] = 1.0
    pick = np.zeros((SLICES * 16, 2 * 6 * WIDE), np.float32)
    for i in range(2):
        for m in range(6):
            for w in range(WIDE):
                pick[(w // 16) * 16 + 2 * m + i, (i * 6 + m) * WIDE + w] = 1.0
    return spread, rep, pick


def lane_iota(rows, lanes):
    return lax.broadcasted_iota(jnp.int32, (rows, lanes), 1)


def poly_sin(x):
    x2 = x * x
    return x * (1.0 + x2 * (-1.0 / 6 + x2 * (1.0 / 120 + x2 * (-1.0 / 5040 + x2 * (1.0 / 362880)))))


def poly_cos(x):
    x2 = x * x
    return 1.0 + x2 * (-0.5 + x2 * (1.0 / 24 + x2 * (-1.0 / 720 + x2 * (1.0 / 40320 - x2 * (1.0 / 3628800)))))


def tap_weights(frac):
    near = jnp.minimum(frac, 1.0 - frac) * (math.pi / 2)
    full = 2.0 * poly_sin(near) * poly_cos(near)
    phi = frac * (math.pi / 4)
    sin_a, cos_a = poly_sin(phi), poly_cos(phi)
    rest = (1.0 - frac) * (math.pi / 4)
    sin_b, cos_b = poly_sin(rest), poly_cos(rest)
    quarter = {-3: -sin_b, -2: -cos_a, -1: -cos_b, 0: -sin_a, 1: sin_b, 2: cos_a, 3: cos_b, 4: sin_a}
    weights = []
    for k in range(TAPS):
        n = k - 3
        t = n - frac
        sign = 1.0 if n % 2 else -1.0
        if n in (0, 1):
            small = jnp.abs(t) < 1e-5
            inverse = 1.0 / jnp.where(small, 1.0, t)
            product = (full * inverse) * (quarter[n] * inverse) * (sign * 4.0 / math.pi**2)
            weights.append(jnp.where(small, 1.0, product))
        else:
            inverse = 1.0 / t
            weights.append((full * inverse) * (quarter[n] * inverse) * (sign * 4.0 / math.pi**2))
    return weights


def wide_lines(values):
    return jnp.concatenate([values, jnp.zeros((values.shape[0], SPAN - LINES), F32)], axis=1)


def left(values, count):
    return pltpu.roll(values, (SPAN - count) % SPAN, 1) if count % SPAN else values


def split3(values):
    high = values.astype(BF16)
    rest = values - high.astype(F32)
    middle = rest.astype(BF16)
    low = (rest - middle.astype(F32)).astype(BF16)
    return high, middle, low


def dot(a, b):
    return jnp.dot(a, b, preferred_element_type=F32)


def dot_first(a, b):
    return lax.dot_general(a, b, (((0,), (0,)), ((), ())), preferred_element_type=F32)


def step_scalars(rr, ra, aa, ab):
    alpha = rr / (penalty * rr + ra)
    rho = ra / rr
    qq = jnp.maximum(aa - rho * ra, 0.0)
    qaq = ab - 2.0 * rho * aa + rho * rho * ra
    next_rr = alpha * alpha * qq
    beta = next_rr / rr
    direction_sq = next_rr + beta * beta * rr
    direction_a = alpha * alpha * qaq - 2.0 * beta * alpha * qq + beta * beta * ra
    image = jnp.maximum(penalty * direction_sq + direction_a, penalty * direction_sq)
    second = jnp.where(image > 0.0, next_rr / jnp.where(image > 0.0, image, 1.0), 0.0)
    return alpha + second * (alpha * rho + beta), -second * alpha


def whole_body(
    prior_ref, maps_ref, start_ref, mask_ref, kspace_any, frac_any, table_any, turned_any, place_any, order_any,
    spread_any, rep_any, pick_any,
    solution_ref, denoised_ref,
    kspace_ref, frac_ref, table_ref, turned_ref, place_ref, order_ref, spread_ref, rep_ref, pick_ref,
    send_maps, got_ref, edge_ref, maps3_ref, weight_ref, data_ref, start_rows_ref,
    send_fields, got_fields, near_sum, far_sum, send_halo, got_halo,
    load_sem, maps_sem, edge_send, edge_recv, field_sem, near_sem, far_sem, halo_send, halo_recv,
):
    me = lax.axis_index("wide")
    nme = lax.axis_index("narrow")
    my_slice = me // 16
    both = 2 * COLS
    barrier = pltpu.get_barrier_semaphore()

    @pl.loop(1, WIDE)
    def _(k):
        pl.semaphore_signal(barrier, inc=1, device_id={"wide": lax.rem(me + k, WIDE)}, device_id_type=MESH)

    @pl.loop(1, NARROW)
    def _(k):
        pl.semaphore_signal(barrier, inc=1, device_id={"narrow": lax.rem(nme + k, NARROW)}, device_id_type=MESH)

    sources = (kspace_any, frac_any, table_any, turned_any, place_any, order_any, spread_any, rep_any, pick_any)
    targets = (kspace_ref, frac_ref, table_ref, turned_ref, place_ref, order_ref, spread_ref, rep_ref, pick_ref)
    loads = [pltpu.make_async_copy(a, b, load_sem.at[i]) for i, (a, b) in enumerate(zip(sources, targets))]
    for load in loads:
        load.start()

    lane8 = lane_iota(8, 128)
    stacked = [jnp.concatenate([prior_ref[t], prior_ref[3 + t]], axis=0) for t in range(3)]
    for q in range(16):
        packed = jnp.zeros((8, 128), F32)
        for t in range(3):
            turned = pltpu.roll(stacked[t], (24 * t - 24 * q) % READOUT, 1)[:, :128]
            packed = jnp.where((lane8 >= 24 * t) & (lane8 < 24 * t + 24), turned, packed)
        high = packed.astype(BF16).astype(F32)
        rest = packed - high
        middle = rest.astype(BF16).astype(F32)
        low = rest - middle
        packed = jnp.concatenate([high, middle, low], axis=1)
        for s in range(SLICES):
            d = 16 * s + q
            block = maps_ref[:, d * 384 : (d + 1) * 384].astype(F32)
            message = jnp.concatenate([block, packed[s : s + 1], packed[4 + s : 5 + s]], axis=0)
            send_maps[d] = message.astype(BF16)

    pl.semaphore_wait(barrier, WIDE + NARROW - 2)

    def to_wide(k, source, target, sems):
        to = lax.rem(me + k, WIDE)
        pltpu.make_async_remote_copy(
            src_ref=source(to), dst_ref=target, send_sem=sems.at[0], recv_sem=sems.at[1],
            device_id={"wide": to}, device_id_type=MESH,
        ).start()

    def finish(source, target, sems, count):
        others = pl.ds(0, count)
        pltpu.make_async_copy(source.at[others], source.at[others], sems.at[0]).wait()
        pltpu.make_async_copy(target.at[others], target.at[others], sems.at[1]).wait()

    @pl.loop(1, WIDE)
    def _(k):
        to_wide(k, lambda to: send_maps.at[to], got_ref.at[me], maps_sem)

    got_ref[me] = send_maps[me]

    edges = [
        pltpu.make_async_remote_copy(
            src_ref=prior_ref.at[pl.ds(first, EDGE)], dst_ref=edge_ref.at[side],
            send_sem=edge_send.at[side], recv_sem=edge_recv.at[side],
            device_id={"wide": lax.rem(me + step, WIDE)}, device_id_type=MESH,
        )
        for side, first, step in ((0, ROWS - EDGE, 1), (1, 0, WIDE - 1))
    ]
    for edge in edges:
        edge.start()

    starts = []
    diagonal = lax.broadcasted_iota(jnp.int32, (COLS, COLS), 0) == lax.broadcasted_iota(jnp.int32, (COLS, COLS), 1)
    for p in range(2):
        row = jnp.broadcast_to(start_ref[p : p + 1, :].astype(F32), (COLS, COLS))
        starts.append(jnp.sum(jnp.where(diagonal, row, 0.0), axis=1, keepdims=True))
    ahead = jnp.concatenate(starts, axis=0).astype(jnp.int32) + 12
    start_rows_ref[...] = jnp.broadcast_to(ahead, (both, SPAN))

    loads[1].wait()
    frac = jnp.concatenate([frac_ref[0], frac_ref[1]], axis=0)
    for k, weight in enumerate(tap_weights(frac)):
        weight_ref[k] = weight

    shot = lax.rem(lane_iota(1, LINES), SHOTS)
    masks = []
    for p in range(2):
        row = jnp.zeros((1, LINES), F32)
        for h in range(SHOTS):
            row = jnp.where(shot == h, mask_ref[p, my_slice, h].astype(F32), row)
        masks.append(row)
    loads[3].wait()
    turned = turned_ref[...].astype(F32)
    forward = [(turned * masks[p]).astype(BF16) for p in range(2)]
    loads[0].wait()
    for p in range(2):
        data_ref[p] = lax.dot_general(
            kspace_ref[p], forward[p], (((0,), (1,)), ((), ())), preferred_element_type=F32
        )
    for i in (2, 4, 5, 6, 7, 8):
        loads[i].wait()

    finish(send_maps, got_ref, maps_sem, WIDE - 1)
    got = got_ref[...].reshape(WIDE * 8, LINES)
    laid = dot_first(got, place_ref[...])
    maps3_ref[...] = laid[:, :LINES].reshape(COLS, COILS, LINES)
    pieces = []
    for m in range(PIECES):
        parts = [laid[m * 128 + 24 * t : m * 128 + 24 * t + 24, LINES:] for t in range(3)]
        pieces.append(jnp.concatenate(parts, axis=1))
    ordered = dot(jnp.concatenate(pieces, axis=0).astype(BF16), order_ref[...])
    prior = ordered[:COLS] + ordered[COLS : 2 * COLS] + ordered[2 * COLS :]

    def bit_set(bit):
        return ((start_rows_ref[...] >> bit) & 1) == 1

    def band_apply(field):
        value = wide_lines(jnp.concatenate([field, field], axis=0))
        value = left(value, -15)
        for bit in range(BAND_BITS):
            value = jnp.where(bit_set(bit), left(value, 1 << bit), value)
        total = jnp.zeros((both, LINES), F32)
        for k in range(TAPS):
            total = total + weight_ref[k] * left(value, k)[:, :LINES]
        return total

    def band_adjoint(values):
        total = jnp.zeros((both, SPAN), F32)
        for k in range(TAPS):
            total = total + left(wide_lines(weight_ref[k] * values), -k)
        for bit in range(BAND_BITS):
            total = jnp.where(bit_set(bit), left(total, -(1 << bit)), total)
        total = left(total, 15)
        return (total[:COLS] + total[COLS:])[:, :LINES]

    def spectra(moved, p):
        image = maps3_ref[...] * moved[p * COLS : (p + 1) * COLS][:, None, :]
        return dot(image.reshape(COLS * COILS, LINES).astype(BF16), forward[p])

    def combine(back):
        return jnp.sum(back.reshape(COLS, COILS, LINES) * maps3_ref[...], axis=1)

    def through(field):
        moved = band_apply(field)
        return [dot(spectra(moved, p).astype(BF16), table_ref[...]) for p in range(2)]

    back = through(prior)
    residue = band_adjoint(jnp.concatenate([combine(data_ref[p] - back[p]) for p in range(2)], axis=0))
    back = through(residue)
    first = band_adjoint(jnp.concatenate([combine(back[p]) for p in range(2)], axis=0))

    fields = jnp.concatenate([residue, first, jnp.zeros((128 - 2 * COLS, LINES), F32)], axis=0)
    high = fields.astype(BF16)
    low = (fields - high.astype(F32)).astype(BF16)
    across = (((1,), (1,)), ((), ()))
    placed = lax.dot_general(spread_ref[...], high, across, preferred_element_type=F32)
    placed = placed + lax.dot_general(spread_ref[...], low, across, preferred_element_type=F32)
    lane = lane_iota(WIDE, 128)
    for row in range(DENSE):
        packed = jnp.zeros((WIDE, 128), F32)
        for i in range(PLACES):
            begin = 48 * i - 128 * row
            if begin < 128 and begin + 48 > 0:
                turned = placed[i * WIDE : (i + 1) * WIDE]
                if begin % 128:
                    turned = pltpu.roll(turned, begin % 128, 1)
                packed = jnp.where((lane >= begin) & (lane < begin + 48), turned, packed)
        send_fields[:, row, :] = packed

    @pl.loop(1, WIDE)
    def _(k):
        to_wide(k, lambda to: send_fields.at[to], got_fields.at[me], field_sem)

    got_fields[me] = send_fields[me]

    moved = band_apply(first)
    squares = jnp.zeros((1, LINES), F32)
    for p in range(2):
        here = spectra(moved, p)
        squares = squares + jnp.sum(here * here.astype(BF16).astype(F32), axis=0, keepdims=True)

    def total(values):
        return jnp.sum(jnp.sum(values, axis=0, keepdims=True), axis=1, keepdims=True)

    lane1 = lane_iota(1, 128)
    sums = jnp.zeros((1, 128), F32)
    for i, part in enumerate((residue * residue, residue * first, first * first, squares)):
        sums = jnp.where(lane1 == i, total(part), sums)
    near_sum[nme] = sums

    @pl.loop(1, NARROW)
    def _(k):
        to = lax.rem(nme + k, NARROW)
        pltpu.make_async_remote_copy(
            src_ref=near_sum.at[nme], dst_ref=near_sum.at[nme], send_sem=near_sem.at[0], recv_sem=near_sem.at[1],
            device_id={"narrow": to}, device_id_type=MESH,
        ).start()

    for edge in edges:
        edge.wait()
    below = jnp.where(me > 0, 1.0, 0.0).astype(F32)
    above = jnp.where(me < WIDE - 1, 1.0, 0.0).astype(F32)
    cells = []
    for s in range(SLICES):
        rows = [edge_ref[0, i, s : s + 1, :] * below for i in range(EDGE)]
        rows += [prior_ref[i, s : s + 1, :] for i in range(ROWS)]
        rows += [edge_ref[1, i, s : s + 1, :] * above for i in range(EDGE)]
        rows += [jnp.zeros((16 - PLACES, READOUT), F32)]
        cells.append(jnp.concatenate(rows, axis=0))

    finish(near_sum, near_sum, near_sem, NARROW - 1)
    far_sum[me] = jnp.sum(near_sum[...].reshape(NARROW, 128), axis=0, keepdims=True)

    @pl.loop(1, WIDE)
    def _(k):
        to_wide(k, lambda to: far_sum.at[me], far_sum.at[me], far_sem)

    finish(far_sum, far_sum, far_sem, WIDE - 1)
    sums = jnp.sum(far_sum[...].reshape(WIDE, 128), axis=0, keepdims=True)
    picked = [jnp.sum(jnp.where(lane1 == i, sums, 0.0), axis=1, keepdims=True) for i in range(4)]
    c0, c1 = step_scalars(*picked)
    solution_ref[...] = prior + c0 * residue + c1 * first

    finish(send_fields, got_fields, field_sem, WIDE - 1)
    lines = [got_fields[:, row, :] for row in range(DENSE)]
    pairs = []
    for m in range(6):
        begin = 96 * m
        row, off = begin // 128, begin % 128
        pair = pltpu.roll(lines[row], 128 - off, 1) if off else lines[row]
        if off + 96 > 128:
            pair = jnp.where(lane < 128 - off, pair, pltpu.roll(lines[row + 1], 128 - off, 1))
        pairs.append(pair)
    pairs = jnp.concatenate(pairs, axis=0)
    joined = c0 * pairs + c1 * pltpu.roll(pairs, 128 - COLS, 1)
    high = joined.astype(BF16)
    low = (joined - high.astype(F32)).astype(BF16)
    block_of = lax.broadcasted_iota(jnp.int32, (16, 2 * READOUT), 0)
    readout_of = lax.rem(lane_iota(16, 2 * READOUT), READOUT)
    inside = (readout_of >= COLS * block_of) & (readout_of < COLS * block_of + COLS)
    change = jnp.zeros((SLICES * 16, READOUT), F32)
    for part in (high, low):
        wide = dot(part, rep_ref[...]).reshape(6 * SLICES, 16, 2 * READOUT)
        wide = jnp.where(inside[None], wide, 0.0).reshape(6 * WIDE, 2 * READOUT).astype(BF16)
        wide = jnp.concatenate([wide[:, :READOUT], wide[:, READOUT:]], axis=0)
        change = change + dot(pick_ref[...], wide)
    cells = [cells[s] + change[16 * s : 16 * s + 16] for s in range(SLICES)]

    def diamond(near, middle, far):
        rows = jnp.concatenate([near[1:11], middle[2:10], far[3:9]], axis=0)
        return rows.astype(BF16)

    send_halo[0] = diamond(cells[3], cells[2], cells[1])
    send_halo[1] = diamond(cells[0], cells[1], cells[2])
    halos = [
        pltpu.make_async_remote_copy(
            src_ref=send_halo.at[side], dst_ref=got_halo.at[side],
            send_sem=halo_send.at[side], recv_sem=halo_recv.at[side],
            device_id={"narrow": lax.rem(nme + step, NARROW)}, device_id_type=MESH,
        )
        for side, step in ((0, 1), (1, NARROW - 1))
    ]
    for halo in halos:
        halo.start()
    for halo in halos:
        halo.wait()

    def opened(side, keep):
        rows = got_halo[side].astype(F32) * keep
        zero = jnp.zeros((8, READOUT), F32)
        near = jnp.concatenate([zero[:1], rows[:10], zero[:5]], axis=0)
        middle = jnp.concatenate([zero[:2], rows[10:18], zero[:6]], axis=0)
        far = jnp.concatenate([zero[:3], rows[18:24], zero[:7]], axis=0)
        return near, middle, far

    has_low = jnp.where(nme > 0, 1.0, 0.0).astype(F32)
    has_high = jnp.where(nme < NARROW - 1, 1.0, 0.0).astype(F32)
    near_low, mid_low, far_low = opened(0, has_low)
    near_high, mid_high, far_high = opened(1, has_high)
    volume = [far_low, mid_low, near_low] + cells + [near_high, mid_high, far_high]
    keeps = [has_low] * 3 + [None] * SLICES + [has_high] * 3
    margin = jnp.zeros((16, 128), F32)
    volume = [jnp.concatenate([one, margin], axis=1) for one in volume]
    line_of = lax.broadcasted_iota(jnp.int32, (16, READOUT + 128), 0) + (ROWS * me - EDGE)
    in_grid = (line_of >= 0) & (line_of < LINES) & (lane_iota(16, READOUT + 128) < READOUT)
    in_grid = in_grid.astype(F32)

    def flux(jump):
        return jump / (1.0 + jump * jump)

    for step in range(DIFF_STEPS):
        last = len(volume) - 1
        across_slices = [flux(volume[i + 1] - volume[i]) for i in range(last)]
        after = []
        for i in range(1, last):
            one = volume[i]
            down = flux(pltpu.roll(one, 15, 0) - one)
            along = flux(pltpu.roll(one, SPAN - 1, 1) - one)
            moved = axis_weights[0] * (down - pltpu.roll(down, 1, 0))
            moved = moved + axis_weights[1] * (across_slices[i] - across_slices[i - 1])
            moved = moved + axis_weights[2] * (along - pltpu.roll(along, 1, 1))
            grid = in_grid if keeps[i] is None else in_grid * keeps[i]
            after.append((one + time_step * moved) * grid)
        volume = after
        keeps = keeps[1:-1]
    for s in range(SLICES):
        for i in range(ROWS):
            denoised_ref[i, s : s + 1, :] = volume[s][EDGE + i : EDGE + i + 1, :READOUT]


def whole(prior, coil_maps, kspace, band_start, frac, mask):
    vmem = pl.BlockSpec(memory_space=pltpu.VMEM)
    smem = pl.BlockSpec(memory_space=pltpu.SMEM)
    far = pl.BlockSpec(memory_space=pl.ANY)
    table = cosine_table()
    constants = (table, table.T) + place_tables() + return_tables()
    constants = [jnp.asarray(one, BF16) for one in constants]
    moved = [kspace, frac] + constants
    return pl.pallas_call(
        whole_body,
        out_shape=(
            jax.ShapeDtypeStruct((COLS, LINES), F32),
            jax.ShapeDtypeStruct((ROWS, SLICES, READOUT), F32),
        ),
        in_specs=[vmem, vmem, vmem, smem] + [far] * len(moved),
        out_specs=(vmem, vmem),
        scratch_shapes=[pltpu.VMEM(one.shape, one.dtype) for one in moved]
        + [
            pltpu.VMEM((WIDE, 8, LINES), BF16),
            pltpu.VMEM((WIDE, 8, LINES), BF16),
            pltpu.VMEM((2, EDGE, SLICES, READOUT), F32),
            pltpu.VMEM((COLS, COILS, LINES), F32),
            pltpu.VMEM((TAPS, 2 * COLS, LINES), F32),
            pltpu.VMEM((2, COLS * COILS, LINES), F32),
            pltpu.VMEM((2 * COLS, SPAN), jnp.int32),
            pltpu.VMEM((WIDE, DENSE, 128), F32),
            pltpu.VMEM((WIDE, DENSE, 128), F32),
            pltpu.VMEM((NARROW, 1, 128), F32),
            pltpu.VMEM((WIDE, 1, 128), F32),
            pltpu.VMEM((2, HALO, READOUT), BF16),
            pltpu.VMEM((2, HALO, READOUT), BF16),
            pltpu.SemaphoreType.DMA((len(moved),)),
            pltpu.SemaphoreType.DMA((2,)),
            pltpu.SemaphoreType.DMA((2,)),
            pltpu.SemaphoreType.DMA((2,)),
            pltpu.SemaphoreType.DMA((2,)),
            pltpu.SemaphoreType.DMA((2,)),
            pltpu.SemaphoreType.DMA((2,)),
            pltpu.SemaphoreType.DMA((2,)),
            pltpu.SemaphoreType.DMA((2,)),
        ],
        compiler_params=pltpu.CompilerParams(collective_id=0, has_side_effects=True, vmem_limit_bytes=48 << 20),
        name="whole",
    )(prior, coil_maps, band_start, mask, *moved)


def per_device(prior, coil_maps, kspace, band_start, band_frac, shot_mask):
    solved, denoised = whole(
        prior, coil_maps, kspace, band_start, jnp.transpose(band_frac, (0, 2, 1)), jnp.transpose(shot_mask, (0, 2, 1))
    )
    return jnp.transpose(solved), denoised


def solution(mesh):
    in_specs = (
        P("wide", "narrow", None),
        P("wide", "narrow"),
        P(None, None, ("narrow", "wide")),
        P(None, ("narrow", "wide")),
        P(None, None, ("narrow", "wide")),
        P(None, None, "narrow"),
    )
    out_specs = (P(None, ("narrow", "wide")), P("wide", "narrow", None))
    return jax.shard_map(per_device, mesh=mesh, in_specs=in_specs, out_specs=out_specs, check_vma=False)
```

```python
import functools
import math

import jax
import jax.numpy as jnp
import numpy as np
from jax import lax
from jax.experimental import pallas as pl
from jax.experimental.pallas import tpu as pltpu
from jax.sharding import PartitionSpec as P

SHOTS = 6
TAPS = 8
DIFF_STEPS = 3
COILS = 16
WIDE = 64
NARROW = 8
LINES = 384
COLS = 24
ROWS = 6
SLICES = 4
READOUT = 384
SPAN = 512
PIECES = 3
EDGE = DIFF_STEPS
PLACES = ROWS + 2 * EDGE
DENSE = 5
HALO = 24
BAND_BITS = 5

penalty = 0.5
time_step = 0.18
axis_weights = (1.0, 0.5, 1.0)

F32 = jnp.float32
BF16 = jnp.bfloat16
MESH = pl.DeviceIdType.MESH


def cosine_table():
    freq = np.arange(LINES, dtype=np.float32)[:, None]
    cell = np.arange(LINES, dtype=np.float32)[None, :]
    angle = np.float32(math.pi) * (cell + np.float32(0.5)) * freq / np.float32(LINES)
    entries = np.cos(angle).astype(np.float32) * np.float32(math.sqrt(2.0 / LINES))
    entries = entries * np.where(freq == 0.0, np.float32(math.sqrt(0.5)), np.float32(1.0))
    return entries.astype(np.float32)


def place_tables():
    place = np.zeros((WIDE * 8, LINES + 128), np.float32)
    for w in range(WIDE):
        for i in range(ROWS):
            place[8 * w + i, ROWS * w + i] = 1.0
        for g in range(2):
            place[8 * w + 6 + g, LINES + g * 64 + w] = 1.0
    order = np.zeros((3 * 128, LINES), np.float32)
    for t in range(3):
        for g in range(2):
            for w in range(WIDE):
                order[t * 128 + g * 64 + w, ROWS * w + 3 * g + t] = 1.0
    return place, order


def return_tables():
    spread = np.zeros((PLACES * WIDE, LINES), np.float32)
    for i in range(PLACES):
        for w in range(WIDE):
            line = ROWS * w - EDGE + i
            if 0 <= line < LINES:
                spread[i * WIDE + w, line] = 1.0
    rep = np.zeros((128, 2 * READOUT), np.float32)
    for i in range(2):
        for x in range(READOUT):
            rep[48 * i + x % COLS, i * READOUT + x] = 1.0
    pick = np.zeros((SLICES * 16, 2 * 6 * WIDE), np.float32)
    for i in range(2):
        for m in range(6):
            for w in range(WIDE):
                pick[(w // 16) * 16 + 2 * m + i, (i * 6 + m) * WIDE + w] = 1.0
    return spread, rep, pick


def lane_iota(rows, lanes):
    return lax.broadcasted_iota(jnp.int32, (rows, lanes), 1)


def poly_sin(x):
    x2 = x * x
    return x * (1.0 + x2 * (-1.0 / 6 + x2 * (1.0 / 120 + x2 * (-1.0 / 5040 + x2 * (1.0 / 362880)))))


def poly_cos(x):
    x2 = x * x
    return 1.0 + x2 * (-0.5 + x2 * (1.0 / 24 + x2 * (-1.0 / 720 + x2 * (1.0 / 40320 - x2 * (1.0 / 3628800)))))


def tap_weights(frac):
    near = jnp.minimum(frac, 1.0 - frac) * (math.pi / 2)
    full = 2.0 * poly_sin(near) * poly_cos(near)
    phi = frac * (math.pi / 4)
    sin_a, cos_a = poly_sin(phi), poly_cos(phi)
    rest = (1.0 - frac) * (math.pi / 4)
    sin_b, cos_b = poly_sin(rest), poly_cos(rest)
    quarter = {-3: -sin_b, -2: -cos_a, -1: -cos_b, 0: -sin_a, 1: sin_b, 2: cos_a, 3: cos_b, 4: sin_a}
    weights = []
    for k in range(TAPS):
        n = k - 3
        t = n - frac
        sign = 1.0 if n % 2 else -1.0
        if n in (0, 1):
            small = jnp.abs(t) < 1e-5
            inverse = 1.0 / jnp.where(small, 1.0, t)
            product = (full * inverse) * (quarter[n] * inverse) * (sign * 4.0 / math.pi**2)
            weights.append(jnp.where(small, 1.0, product))
        else:
            inverse = 1.0 / t
            weights.append((full * inverse) * (quarter[n] * inverse) * (sign * 4.0 / math.pi**2))
    return weights


def wide_lines(values):
    return jnp.concatenate([values, jnp.zeros((values.shape[0], SPAN - LINES), F32)], axis=1)


def left(values, count):
    return pltpu.roll(values, (SPAN - count) % SPAN, 1) if count % SPAN else values


def split3(values):
    high = values.astype(BF16)
    rest = values - high.astype(F32)
    middle = rest.astype(BF16)
    low = (rest - middle.astype(F32)).astype(BF16)
    return high, middle, low


def dot(a, b):
    return jnp.dot(a, b, preferred_element_type=F32)


def dot_first(a, b):
    return lax.dot_general(a, b, (((0,), (0,)), ((), ())), preferred_element_type=F32)


def step_scalars(rr, ra, aa, ab):
    alpha = rr / (penalty * rr + ra)
    rho = ra / rr
    qq = jnp.maximum(aa - rho * ra, 0.0)
    qaq = ab - 2.0 * rho * aa + rho * rho * ra
    next_rr = alpha * alpha * qq
    beta = next_rr / rr
    direction_sq = next_rr + beta * beta * rr
    direction_a = alpha * alpha * qaq - 2.0 * beta * alpha * qq + beta * beta * ra
    image = jnp.maximum(penalty * direction_sq + direction_a, penalty * direction_sq)
    second = jnp.where(image > 0.0, next_rr / jnp.where(image > 0.0, image, 1.0), 0.0)
    return alpha + second * (alpha * rho + beta), -second * alpha


def whole_body(
    mask_any, kspace_any, frac_any, table_any, turned_any, place_any, order_any,
    spread_any, rep_any, pick_any, prior_any, maps_any, start_any,
    solution_ref, denoised_ref,
    mask_ref, kspace_ref, frac_ref, table_ref, turned_ref, place_ref, order_ref, spread_ref, rep_ref, pick_ref,
    prior_ref, maps_ref, start_ref,
    send_maps, got_ref, edge_ref, maps3_ref, weight_ref, data_ref, start_rows_ref,
    send_fields, got_fields, near_sum, far_sum, send_halo, got_halo,
    load_sem, maps_sem, edge_send, edge_recv, field_sem, near_sem, far_sem, halo_send, halo_recv,
):
    me = lax.axis_index("wide")
    nme = lax.axis_index("narrow")
    my_slice = me // 16
    both = 2 * COLS
    barrier = pltpu.get_barrier_semaphore()

    sources = (
        kspace_any, frac_any, table_any, turned_any, place_any, order_any, spread_any, rep_any, pick_any,
        prior_any, maps_any, start_any, mask_any,
    )
    targets = (
        kspace_ref, frac_ref, table_ref, turned_ref, place_ref, order_ref, spread_ref, rep_ref, pick_ref,
        prior_ref, maps_ref, start_ref, mask_ref,
    )
    loads = [pltpu.make_async_copy(a, b, load_sem.at[i]) for i, (a, b) in enumerate(zip(sources, targets))]
    for i in (9, 10, 11, 12, 1, 3, 0, 2, 4, 5, 6, 7, 8):
        loads[i].start()

    @pl.loop(1, WIDE)
    def _(k):
        pl.semaphore_signal(barrier, inc=1, device_id={"wide": lax.rem(me + k, WIDE)}, device_id_type=MESH)

    @pl.loop(1, NARROW)
    def _(k):
        pl.semaphore_signal(barrier, inc=1, device_id={"narrow": lax.rem(nme + k, NARROW)}, device_id_type=MESH)


    loads[9].wait()
    loads[10].wait()
    lane8 = lane_iota(8, 128)
    stacked = [jnp.concatenate([prior_ref[t], prior_ref[3 + t]], axis=0) for t in range(3)]
    for q in range(16):
        packed = jnp.zeros((8, 128), F32)
        for t in range(3):
            turned = pltpu.roll(stacked[t], (24 * t - 24 * q) % READOUT, 1)[:, :128]
            packed = jnp.where((lane8 >= 24 * t) & (lane8 < 24 * t + 24), turned, packed)
        high = packed.astype(BF16).astype(F32)
        rest = packed - high
        middle = rest.astype(BF16).astype(F32)
        low = rest - middle
        packed = jnp.concatenate([high, middle, low], axis=1)
        for s in range(SLICES):
            d = 16 * s + q
            block = maps_ref[:, d * 384 : (d + 1) * 384].astype(F32)
            message = jnp.concatenate([block, packed[s : s + 1], packed[4 + s : 5 + s]], axis=0)
            send_maps[d] = message.astype(BF16)

    pl.semaphore_wait(barrier, WIDE + NARROW - 2)

    def to_wide(k, source, target, sems):
        to = lax.rem(me + k, WIDE)
        pltpu.make_async_remote_copy(
            src_ref=source(to), dst_ref=target, send_sem=sems.at[0], recv_sem=sems.at[1],
            device_id={"wide": to}, device_id_type=MESH,
        ).start()

    def finish(source, target, sems, count):
        others = pl.ds(0, count)
        pltpu.make_async_copy(source.at[others], source.at[others], sems.at[0]).wait()
        pltpu.make_async_copy(target.at[others], target.at[others], sems.at[1]).wait()

    @pl.loop(1, WIDE)
    def _(k):
        to_wide(k, lambda to: send_maps.at[to], got_ref.at[me], maps_sem)

    got_ref[me] = send_maps[me]

    edges = [
        pltpu.make_async_remote_copy(
            src_ref=prior_ref.at[pl.ds(first, EDGE)], dst_ref=edge_ref.at[side],
            send_sem=edge_send.at[side], recv_sem=edge_recv.at[side],
            device_id={"wide": lax.rem(me + step, WIDE)}, device_id_type=MESH,
        )
        for side, first, step in ((0, ROWS - EDGE, 1), (1, 0, WIDE - 1))
    ]
    for edge in edges:
        edge.start()

    loads[11].wait()
    loads[12].wait()
    starts = []
    diagonal = lax.broadcasted_iota(jnp.int32, (COLS, COLS), 0) == lax.broadcasted_iota(jnp.int32, (COLS, COLS), 1)
    for p in range(2):
        row = jnp.broadcast_to(start_ref[p : p + 1, :].astype(F32), (COLS, COLS))
        starts.append(jnp.sum(jnp.where(diagonal, row, 0.0), axis=1, keepdims=True))
    ahead = jnp.concatenate(starts, axis=0).astype(jnp.int32) + 12
    start_rows_ref[...] = jnp.broadcast_to(ahead, (both, SPAN))

    loads[1].wait()
    frac = jnp.concatenate([frac_ref[0], frac_ref[1]], axis=0)
    for k, weight in enumerate(tap_weights(frac)):
        weight_ref[k] = weight

    shot = lax.rem(lane_iota(1, LINES), SHOTS)
    masks = []
    for p in range(2):
        row = jnp.zeros((1, LINES), F32)
        for h in range(SHOTS):
            row = jnp.where(shot == h, mask_ref[p, my_slice, h].astype(F32), row)
        masks.append(row)
    loads[3].wait()
    turned = turned_ref[...].astype(F32)
    forward = [(turned * masks[p]).astype(BF16) for p in range(2)]
    loads[0].wait()
    for p in range(2):
        data_ref[p] = lax.dot_general(
            kspace_ref[p], forward[p], (((0,), (1,)), ((), ())), preferred_element_type=F32
        )
    for i in (2, 4, 5, 6, 7, 8):
        loads[i].wait()

    finish(send_maps, got_ref, maps_sem, WIDE - 1)
    got = got_ref[...].reshape(WIDE * 8, LINES)
    laid = dot_first(got, place_ref[...])
    maps3_ref[...] = laid[:, :LINES].reshape(COLS, COILS, LINES)
    pieces = []
    for m in range(PIECES):
        parts = [laid[m * 128 + 24 * t : m * 128 + 24 * t + 24, LINES:] for t in range(3)]
        pieces.append(jnp.concatenate(parts, axis=1))
    ordered = dot(jnp.concatenate(pieces, axis=0).astype(BF16), order_ref[...])
    prior = ordered[:COLS] + ordered[COLS : 2 * COLS] + ordered[2 * COLS :]

    def bit_set(bit):
        return ((start_rows_ref[...] >> bit) & 1) == 1

    def band_apply(field):
        value = wide_lines(jnp.concatenate([field, field], axis=0))
        value = left(value, -15)
        for bit in range(BAND_BITS):
            value = jnp.where(bit_set(bit), left(value, 1 << bit), value)
        total = jnp.zeros((both, LINES), F32)
        for k in range(TAPS):
            total = total + weight_ref[k] * left(value, k)[:, :LINES]
        return total

    def band_adjoint(values):
        total = jnp.zeros((both, SPAN), F32)
        for k in range(TAPS):
            total = total + left(wide_lines(weight_ref[k] * values), -k)
        for bit in range(BAND_BITS):
            total = jnp.where(bit_set(bit), left(total, -(1 << bit)), total)
        total = left(total, 15)
        return (total[:COLS] + total[COLS:])[:, :LINES]

    def spectra(moved, p):
        image = maps3_ref[...] * moved[p * COLS : (p + 1) * COLS][:, None, :]
        return dot(image.reshape(COLS * COILS, LINES).astype(BF16), forward[p])

    def combine(back):
        return jnp.sum(back.reshape(COLS, COILS, LINES) * maps3_ref[...], axis=1)

    def through(field):
        moved = band_apply(field)
        return [dot(spectra(moved, p).astype(BF16), table_ref[...]) for p in range(2)]

    back = through(prior)
    residue = band_adjoint(jnp.concatenate([combine(data_ref[p] - back[p]) for p in range(2)], axis=0))
    back = through(residue)
    first = band_adjoint(jnp.concatenate([combine(back[p]) for p in range(2)], axis=0))

    fields = jnp.concatenate([residue, first, jnp.zeros((128 - 2 * COLS, LINES), F32)], axis=0)
    high = fields.astype(BF16)
    low = (fields - high.astype(F32)).astype(BF16)
    across = (((1,), (1,)), ((), ()))
    placed = lax.dot_general(spread_ref[...], high, across, preferred_element_type=F32)
    placed = placed + lax.dot_general(spread_ref[...], low, across, preferred_element_type=F32)
    lane = lane_iota(WIDE, 128)
    for row in range(DENSE):
        packed = jnp.zeros((WIDE, 128), F32)
        for i in range(PLACES):
            begin = 48 * i - 128 * row
            if begin < 128 and begin + 48 > 0:
                turned = placed[i * WIDE : (i + 1) * WIDE]
                if begin % 128:
                    turned = pltpu.roll(turned, begin % 128, 1)
                packed = jnp.where((lane >= begin) & (lane < begin + 48), turned, packed)
        send_fields[:, row, :] = packed

    @pl.loop(1, WIDE)
    def _(k):
        to_wide(k, lambda to: send_fields.at[to], got_fields.at[me], field_sem)

    got_fields[me] = send_fields[me]

    moved = band_apply(first)
    squares = jnp.zeros((1, LINES), F32)
    for p in range(2):
        here = spectra(moved, p)
        squares = squares + jnp.sum(here * here.astype(BF16).astype(F32), axis=0, keepdims=True)

    def total(values):
        return jnp.sum(jnp.sum(values, axis=0, keepdims=True), axis=1, keepdims=True)

    lane1 = lane_iota(1, 128)
    sums = jnp.zeros((1, 128), F32)
    for i, part in enumerate((residue * residue, residue * first, first * first, squares)):
        sums = jnp.where(lane1 == i, total(part), sums)
    near_sum[nme] = sums

    @pl.loop(1, NARROW)
    def _(k):
        to = lax.rem(nme + k, NARROW)
        pltpu.make_async_remote_copy(
            src_ref=near_sum.at[nme], dst_ref=near_sum.at[nme], send_sem=near_sem.at[0], recv_sem=near_sem.at[1],
            device_id={"narrow": to}, device_id_type=MESH,
        ).start()

    for edge in edges:
        edge.wait()
    below = jnp.where(me > 0, 1.0, 0.0).astype(F32)
    above = jnp.where(me < WIDE - 1, 1.0, 0.0).astype(F32)
    cells = []
    for s in range(SLICES):
        rows = [edge_ref[0, i, s : s + 1, :] * below for i in range(EDGE)]
        rows += [prior_ref[i, s : s + 1, :] for i in range(ROWS)]
        rows += [edge_ref[1, i, s : s + 1, :] * above for i in range(EDGE)]
        rows += [jnp.zeros((16 - PLACES, READOUT), F32)]
        cells.append(jnp.concatenate(rows, axis=0))

    finish(near_sum, near_sum, near_sem, NARROW - 1)
    far_sum[me] = jnp.sum(near_sum[...].reshape(NARROW, 128), axis=0, keepdims=True)

    @pl.loop(1, WIDE)
    def _(k):
        to_wide(k, lambda to: far_sum.at[me], far_sum.at[me], far_sem)

    finish(far_sum, far_sum, far_sem, WIDE - 1)
    sums = jnp.sum(far_sum[...].reshape(WIDE, 128), axis=0, keepdims=True)
    picked = [jnp.sum(jnp.where(lane1 == i, sums, 0.0), axis=1, keepdims=True) for i in range(4)]
    c0, c1 = step_scalars(*picked)
    solution_ref[...] = prior + c0 * residue + c1 * first

    finish(send_fields, got_fields, field_sem, WIDE - 1)
    lines = [got_fields[:, row, :] for row in range(DENSE)]
    pairs = []
    for m in range(6):
        begin = 96 * m
        row, off = begin // 128, begin % 128
        pair = pltpu.roll(lines[row], 128 - off, 1) if off else lines[row]
        if off + 96 > 128:
            pair = jnp.where(lane < 128 - off, pair, pltpu.roll(lines[row + 1], 128 - off, 1))
        pairs.append(pair)
    pairs = jnp.concatenate(pairs, axis=0)
    joined = c0 * pairs + c1 * pltpu.roll(pairs, 128 - COLS, 1)
    high = joined.astype(BF16)
    low = (joined - high.astype(F32)).astype(BF16)
    block_of = lax.broadcasted_iota(jnp.int32, (16, 2 * READOUT), 0)
    readout_of = lax.rem(lane_iota(16, 2 * READOUT), READOUT)
    inside = (readout_of >= COLS * block_of) & (readout_of < COLS * block_of + COLS)
    change = jnp.zeros((SLICES * 16, READOUT), F32)
    for part in (high, low):
        wide = dot(part, rep_ref[...]).reshape(6 * SLICES, 16, 2 * READOUT)
        wide = jnp.where(inside[None], wide, 0.0).reshape(6 * WIDE, 2 * READOUT).astype(BF16)
        wide = jnp.concatenate([wide[:, :READOUT], wide[:, READOUT:]], axis=0)
        change = change + dot(pick_ref[...], wide)
    cells = [cells[s] + change[16 * s : 16 * s + 16] for s in range(SLICES)]

    def diamond(near, middle, far):
        rows = jnp.concatenate([near[1:11], middle[2:10], far[3:9]], axis=0)
        return rows.astype(BF16)

    send_halo[0] = diamond(cells[3], cells[2], cells[1])
    send_halo[1] = diamond(cells[0], cells[1], cells[2])
    halos = [
        pltpu.make_async_remote_copy(
            src_ref=send_halo.at[side], dst_ref=got_halo.at[side],
            send_sem=halo_send.at[side], recv_sem=halo_recv.at[side],
            device_id={"narrow": lax.rem(nme + step, NARROW)}, device_id_type=MESH,
        )
        for side, step in ((0, 1), (1, NARROW - 1))
    ]
    for halo in halos:
        halo.start()
    for halo in halos:
        halo.wait()

    def opened(side, keep):
        rows = got_halo[side].astype(F32) * keep
        zero = jnp.zeros((8, READOUT), F32)
        near = jnp.concatenate([zero[:1], rows[:10], zero[:5]], axis=0)
        middle = jnp.concatenate([zero[:2], rows[10:18], zero[:6]], axis=0)
        far = jnp.concatenate([zero[:3], rows[18:24], zero[:7]], axis=0)
        return near, middle, far

    has_low = jnp.where(nme > 0, 1.0, 0.0).astype(F32)
    has_high = jnp.where(nme < NARROW - 1, 1.0, 0.0).astype(F32)
    near_low, mid_low, far_low = opened(0, has_low)
    near_high, mid_high, far_high = opened(1, has_high)
    volume = [far_low, mid_low, near_low] + cells + [near_high, mid_high, far_high]
    keeps = [has_low] * 3 + [None] * SLICES + [has_high] * 3
    margin = jnp.zeros((16, 128), F32)
    volume = [jnp.concatenate([one, margin], axis=1) for one in volume]
    line_of = lax.broadcasted_iota(jnp.int32, (16, READOUT + 128), 0) + (ROWS * me - EDGE)
    in_grid = (line_of >= 0) & (line_of < LINES) & (lane_iota(16, READOUT + 128) < READOUT)
    in_grid = in_grid.astype(F32)

    def flux(jump):
        return jump / (1.0 + jump * jump)

    for step in range(DIFF_STEPS):
        last = len(volume) - 1
        across_slices = [flux(volume[i + 1] - volume[i]) for i in range(last)]
        after = []
        for i in range(1, last):
            one = volume[i]
            down = flux(pltpu.roll(one, 15, 0) - one)
            along = flux(pltpu.roll(one, SPAN - 1, 1) - one)
            moved = axis_weights[0] * (down - pltpu.roll(down, 1, 0))
            moved = moved + axis_weights[1] * (across_slices[i] - across_slices[i - 1])
            moved = moved + axis_weights[2] * (along - pltpu.roll(along, 1, 1))
            grid = in_grid if keeps[i] is None else in_grid * keeps[i]
            after.append((one + time_step * moved) * grid)
        volume = after
        keeps = keeps[1:-1]
    for s in range(SLICES):
        for i in range(ROWS):
            denoised_ref[i, s : s + 1, :] = volume[s][EDGE + i : EDGE + i + 1, :READOUT]


def whole(prior, coil_maps, kspace, band_start, frac, mask):
    vmem = pl.BlockSpec(memory_space=pltpu.VMEM)
    far = pl.BlockSpec(memory_space=pltpu.HBM)
    table = cosine_table()
    constants = (table, table.T) + place_tables() + return_tables()
    constants = [jnp.asarray(one, BF16) for one in constants]
    moved = [kspace, frac] + constants + [prior, coil_maps, band_start]
    return pl.pallas_call(
        whole_body,
        out_shape=(
            jax.ShapeDtypeStruct((COLS, LINES), F32),
            jax.ShapeDtypeStruct((ROWS, SLICES, READOUT), F32),
        ),
        in_specs=[far] * (len(moved) + 1),
        out_specs=(vmem, vmem),
        scratch_shapes=[pltpu.SMEM(mask.shape, mask.dtype)]
        + [pltpu.VMEM(one.shape, one.dtype) for one in moved]
        + [
            pltpu.VMEM((WIDE, 8, LINES), BF16),
            pltpu.VMEM((WIDE, 8, LINES), BF16),
            pltpu.VMEM((2, EDGE, SLICES, READOUT), F32),
            pltpu.VMEM((COLS, COILS, LINES), F32),
            pltpu.VMEM((TAPS, 2 * COLS, LINES), F32),
            pltpu.VMEM((2, COLS * COILS, LINES), F32),
            pltpu.VMEM((2 * COLS, SPAN), jnp.int32),
            pltpu.VMEM((WIDE, DENSE, 128), F32),
            pltpu.VMEM((WIDE, DENSE, 128), F32),
            pltpu.VMEM((NARROW, 1, 128), F32),
            pltpu.VMEM((WIDE, 1, 128), F32),
            pltpu.VMEM((2, HALO, READOUT), BF16),
            pltpu.VMEM((2, HALO, READOUT), BF16),
            pltpu.SemaphoreType.DMA((len(moved) + 1,)),
            pltpu.SemaphoreType.DMA((2,)),
            pltpu.SemaphoreType.DMA((2,)),
            pltpu.SemaphoreType.DMA((2,)),
            pltpu.SemaphoreType.DMA((2,)),
            pltpu.SemaphoreType.DMA((2,)),
            pltpu.SemaphoreType.DMA((2,)),
            pltpu.SemaphoreType.DMA((2,)),
            pltpu.SemaphoreType.DMA((2,)),
        ],
        compiler_params=pltpu.CompilerParams(collective_id=0, has_side_effects=True, vmem_limit_bytes=63 << 20),
        name="whole",
    )(mask, *moved)


def per_device(prior, coil_maps, kspace, band_start, band_frac, shot_mask):
    solved, denoised = whole(
        prior, coil_maps, kspace, band_start, jnp.transpose(band_frac, (0, 2, 1)), jnp.transpose(shot_mask, (0, 2, 1))
    )
    return jnp.transpose(solved), denoised


def solution(mesh):
    in_specs = (
        P("wide", "narrow", None),
        P("wide", "narrow"),
        P(None, None, ("narrow", "wide")),
        P(None, ("narrow", "wide")),
        P(None, None, ("narrow", "wide")),
        P(None, None, "narrow"),
    )
    out_specs = (P(None, ("narrow", "wide")), P("wide", "narrow", None))
    return jax.shard_map(per_device, mesh=mesh, in_specs=in_specs, out_specs=out_specs, check_vma=False)
```

```python
import functools
import math

import jax
import jax.numpy as jnp
import numpy as np
from jax import lax
from jax.experimental import pallas as pl
from jax.experimental.pallas import tpu as pltpu
from jax.sharding import PartitionSpec as P

SHOTS = 6
TAPS = 8
DIFF_STEPS = 3
COILS = 16
WIDE = 64
NARROW = 8
PLANE = 32
LINE = 16
LINES = 384
COLS = 24
ROWS = 6
SLICES = 4
READOUT = 384
SPAN = 512
PIECES = 3
EDGE = DIFF_STEPS
PLACES = ROWS + 2 * EDGE
DENSE = 5
HALO = 24
BAND_BITS = 5

penalty = 0.5
time_step = 0.18
axis_weights = (1.0, 0.5, 1.0)

F32 = jnp.float32
BF16 = jnp.bfloat16
MESH = pl.DeviceIdType.MESH


def cosine_table():
    freq = np.arange(LINES, dtype=np.float32)[:, None]
    cell = np.arange(LINES, dtype=np.float32)[None, :]
    angle = np.float32(math.pi) * (cell + np.float32(0.5)) * freq / np.float32(LINES)
    entries = np.cos(angle).astype(np.float32) * np.float32(math.sqrt(2.0 / LINES))
    entries = entries * np.where(freq == 0.0, np.float32(math.sqrt(0.5)), np.float32(1.0))
    return entries.astype(np.float32)


def place_tables():
    place = np.zeros((WIDE * 8, LINES + 128), np.float32)
    for w in range(WIDE):
        for i in range(ROWS):
            place[8 * w + i, ROWS * w + i] = 1.0
        for g in range(2):
            place[8 * w + 6 + g, LINES + g * 64 + w] = 1.0
    order = np.zeros((3 * 128, LINES), np.float32)
    for t in range(3):
        for g in range(2):
            for w in range(WIDE):
                order[t * 128 + g * 64 + w, ROWS * w + 3 * g + t] = 1.0
    return place, order


def return_tables():
    spread = np.zeros((PLACES * WIDE, LINES), np.float32)
    for i in range(PLACES):
        for w in range(WIDE):
            line = ROWS * w - EDGE + i
            if 0 <= line < LINES:
                spread[i * WIDE + w, line] = 1.0
    rep = np.zeros((128, 2 * READOUT), np.float32)
    for i in range(2):
        for x in range(READOUT):
            rep[48 * i + x % COLS, i * READOUT + x] = 1.0
    pick = np.zeros((SLICES * 16, 2 * 6 * WIDE), np.float32)
    for i in range(2):
        for m in range(6):
            for w in range(WIDE):
                pick[(w // 16) * 16 + 2 * m + i, (i * 6 + m) * WIDE + w] = 1.0
    return spread, rep, pick


def lane_iota(rows, lanes):
    return lax.broadcasted_iota(jnp.int32, (rows, lanes), 1)


def poly_sin(x):
    x2 = x * x
    return x * (1.0 + x2 * (-1.0 / 6 + x2 * (1.0 / 120 + x2 * (-1.0 / 5040 + x2 * (1.0 / 362880)))))


def poly_cos(x):
    x2 = x * x
    return 1.0 + x2 * (-0.5 + x2 * (1.0 / 24 + x2 * (-1.0 / 720 + x2 * (1.0 / 40320 - x2 * (1.0 / 3628800)))))


def tap_weights(frac):
    near = jnp.minimum(frac, 1.0 - frac) * (math.pi / 2)
    full = 2.0 * poly_sin(near) * poly_cos(near)
    phi = frac * (math.pi / 4)
    sin_a, cos_a = poly_sin(phi), poly_cos(phi)
    rest = (1.0 - frac) * (math.pi / 4)
    sin_b, cos_b = poly_sin(rest), poly_cos(rest)
    quarter = {-3: -sin_b, -2: -cos_a, -1: -cos_b, 0: -sin_a, 1: sin_b, 2: cos_a, 3: cos_b, 4: sin_a}
    weights = []
    for k in range(TAPS):
        n = k - 3
        t = n - frac
        sign = 1.0 if n % 2 else -1.0
        if n in (0, 1):
            small = jnp.abs(t) < 1e-5
            inverse = 1.0 / jnp.where(small, 1.0, t)
            product = (full * inverse) * (quarter[n] * inverse) * (sign * 4.0 / math.pi**2)
            weights.append(jnp.where(small, 1.0, product))
        else:
            inverse = 1.0 / t
            weights.append((full * inverse) * (quarter[n] * inverse) * (sign * 4.0 / math.pi**2))
    return weights


def wide_lines(values):
    return jnp.concatenate([values, jnp.zeros((values.shape[0], SPAN - LINES), F32)], axis=1)


def left(values, count):
    return pltpu.roll(values, (SPAN - count) % SPAN, 1) if count % SPAN else values


def split3(values):
    high = values.astype(BF16)
    rest = values - high.astype(F32)
    middle = rest.astype(BF16)
    low = (rest - middle.astype(F32)).astype(BF16)
    return high, middle, low


def dot(a, b):
    return jnp.dot(a, b, preferred_element_type=F32)


def dot_first(a, b):
    return lax.dot_general(a, b, (((0,), (0,)), ((), ())), preferred_element_type=F32)


def step_scalars(rr, ra, aa, ab):
    alpha = rr / (penalty * rr + ra)
    rho = ra / rr
    qq = jnp.maximum(aa - rho * ra, 0.0)
    qaq = ab - 2.0 * rho * aa + rho * rho * ra
    next_rr = alpha * alpha * qq
    beta = next_rr / rr
    direction_sq = next_rr + beta * beta * rr
    direction_a = alpha * alpha * qaq - 2.0 * beta * alpha * qq + beta * beta * ra
    image = jnp.maximum(penalty * direction_sq + direction_a, penalty * direction_sq)
    second = jnp.where(image > 0.0, next_rr / jnp.where(image > 0.0, image, 1.0), 0.0)
    return alpha + second * (alpha * rho + beta), -second * alpha


def whole_body(
    mask_any, kspace_any, frac_any, table_any, turned_any, place_any, order_any,
    spread_any, rep_any, pick_any, prior_any, maps_any, start_any,
    solution_ref, denoised_ref,
    mask_ref, kspace_ref, frac_ref, table_ref, turned_ref, place_ref, order_ref, spread_ref, rep_ref, pick_ref,
    prior_ref, maps_ref, start_ref,
    send_maps, got_ref, edge_ref, maps3_ref, weight_ref, data_ref, start_rows_ref,
    send_fields, got_fields, near_sum, far_sum, send_halo, got_halo,
    load_sem, maps_sem, edge_send, edge_recv, field_sem, near_sem, far_sem, halo_send, halo_recv,
):
    me = lax.axis_index("wide")
    nme = lax.axis_index("narrow")
    my_slice = me // 16
    both = 2 * COLS
    z_lo = me // 8
    barrier = pltpu.get_barrier_semaphore()

    def far_first(k):
        step = k // 8
        half = lax.rem(z_lo // 4 + 1 - step // 4 + 2, 2)
        return (4 * half + lax.rem(z_lo + 7 - step, 4)) * 8 + lax.rem(me + 7 - lax.rem(k, 8), 8)

    sources = (
        kspace_any, frac_any, table_any, turned_any, place_any, order_any, spread_any, rep_any, pick_any,
        prior_any, maps_any, start_any, mask_any,
    )
    targets = (
        kspace_ref, frac_ref, table_ref, turned_ref, place_ref, order_ref, spread_ref, rep_ref, pick_ref,
        prior_ref, maps_ref, start_ref, mask_ref,
    )
    loads = [pltpu.make_async_copy(a, b, load_sem.at[i]) for i, (a, b) in enumerate(zip(sources, targets))]
    for i in (9, 10, 11, 12, 1, 3, 0, 2, 4, 5, 6, 7, 8):
        loads[i].start()

    core, y_at = lax.rem(me, 2), lax.rem(me // 2, 4)
    x_at, z_hi = lax.rem(nme, 4), nme // 4
    z_at = z_hi * 8 + z_lo

    def in_plane(a, b, c):
        wide_to = z_lo * 8 + lax.rem(y_at + b, 4) * 2 + lax.rem(core + c, 2)
        return {"wide": wide_to, "narrow": z_hi * 4 + lax.rem(x_at + a, 4)}

    def in_line(a):
        z_to = lax.rem(z_at + a, 16)
        return {"wide": lax.rem(z_to, 8) * 8 + lax.rem(me, 8), "narrow": (z_to // 8) * 4 + x_at}

    plane = [(a, b, c) for a in range(4) for b in range(4) for c in range(2) if (a, b, c) != (0, 0, 0)]
    plane.sort(key=lambda at: -(min(at[0], 4 - at[0]) + min(at[1], 4 - at[1])))
    line = sorted(range(1, 16), key=lambda a: -min(a, 16 - a))

    @pl.loop(1, 8)
    def _(k):
        other = {"wide": lax.rem(me + 8 * k, WIDE), "narrow": (1 - z_hi) * 4 + x_at}
        pl.semaphore_signal(barrier, inc=1, device_id=other, device_id_type=MESH)

    @pl.loop(1, NARROW)
    def _(k):
        pl.semaphore_signal(barrier, inc=1, device_id={"narrow": lax.rem(nme + k, NARROW)}, device_id_type=MESH)

    @pl.loop(0, WIDE - 1)
    def _(k):
        pl.semaphore_signal(barrier, inc=1, device_id={"wide": far_first(k)}, device_id_type=MESH)

    for a, b, c in plane:
        if a and (b or c):
            pl.semaphore_signal(barrier, inc=1, device_id=in_plane(a, b, c), device_id_type=MESH)

    loads[9].wait()
    loads[10].wait()
    lane8 = lane_iota(8, 128)
    stacked = [jnp.concatenate([prior_ref[t], prior_ref[3 + t]], axis=0) for t in range(3)]
    for q in range(16):
        packed = jnp.zeros((8, 128), F32)
        for t in range(3):
            turned = pltpu.roll(stacked[t], (24 * t - 24 * q) % READOUT, 1)[:, :128]
            packed = jnp.where((lane8 >= 24 * t) & (lane8 < 24 * t + 24), turned, packed)
        high = packed.astype(BF16).astype(F32)
        rest = packed - high
        middle = rest.astype(BF16).astype(F32)
        low = rest - middle
        packed = jnp.concatenate([high, middle, low], axis=1)
        for s in range(SLICES):
            d = 16 * s + q
            block = maps_ref[:, d * 384 : (d + 1) * 384].astype(F32)
            message = jnp.concatenate([block, packed[s : s + 1], packed[4 + s : 5 + s]], axis=0)
            send_maps[d] = message.astype(BF16)

    pl.semaphore_wait(barrier, WIDE + NARROW - 2 + 21 + 7)

    def to_wide(to, source, target, sems):
        pltpu.make_async_remote_copy(
            src_ref=source(to), dst_ref=target, send_sem=sems.at[0], recv_sem=sems.at[1],
            device_id={"wide": to}, device_id_type=MESH,
        ).start()

    def finish(source, target, sems, count):
        others = pl.ds(0, count)
        pltpu.make_async_copy(source.at[others], source.at[others], sems.at[0]).wait()
        pltpu.make_async_copy(target.at[others], target.at[others], sems.at[1]).wait()

    @pl.loop(1, WIDE)
    def _(k):
        to_wide(lax.rem(me + k, WIDE), lambda to: send_maps.at[to], got_ref.at[me], maps_sem)

    got_ref[me] = send_maps[me]

    edges = [
        pltpu.make_async_remote_copy(
            src_ref=prior_ref.at[pl.ds(first, EDGE)], dst_ref=edge_ref.at[side],
            send_sem=edge_send.at[side], recv_sem=edge_recv.at[side],
            device_id={"wide": lax.rem(me + step, WIDE)}, device_id_type=MESH,
        )
        for side, first, step in ((0, ROWS - EDGE, 1), (1, 0, WIDE - 1))
    ]
    for edge in edges:
        edge.start()

    loads[11].wait()
    loads[12].wait()
    starts = []
    diagonal = lax.broadcasted_iota(jnp.int32, (COLS, COLS), 0) == lax.broadcasted_iota(jnp.int32, (COLS, COLS), 1)
    for p in range(2):
        row = jnp.broadcast_to(start_ref[p : p + 1, :].astype(F32), (COLS, COLS))
        starts.append(jnp.sum(jnp.where(diagonal, row, 0.0), axis=1, keepdims=True))
    ahead = jnp.concatenate(starts, axis=0).astype(jnp.int32) + 12
    start_rows_ref[...] = jnp.broadcast_to(ahead, (both, SPAN))

    loads[1].wait()
    frac = jnp.concatenate([frac_ref[0], frac_ref[1]], axis=0)
    for k, weight in enumerate(tap_weights(frac)):
        weight_ref[k] = weight

    shot = lax.rem(lane_iota(1, LINES), SHOTS)
    masks = []
    for p in range(2):
        row = jnp.zeros((1, LINES), F32)
        for h in range(SHOTS):
            row = jnp.where(shot == h, mask_ref[p, my_slice, h].astype(F32), row)
        masks.append(row)
    loads[3].wait()
    turned = turned_ref[...].astype(F32)
    forward = [(turned * masks[p]).astype(BF16) for p in range(2)]
    loads[0].wait()
    for p in range(2):
        data_ref[p] = lax.dot_general(
            kspace_ref[p], forward[p], (((0,), (1,)), ((), ())), preferred_element_type=F32
        )
    for i in (2, 4, 5, 6, 7, 8):
        loads[i].wait()

    finish(send_maps, got_ref, maps_sem, WIDE - 1)
    got = got_ref[...].reshape(WIDE * 8, LINES)
    laid = dot_first(got, place_ref[...])
    maps3_ref[...] = laid[:, :LINES].reshape(COLS, COILS, LINES)
    pieces = []
    for m in range(PIECES):
        parts = [laid[m * 128 + 24 * t : m * 128 + 24 * t + 24, LINES:] for t in range(3)]
        pieces.append(jnp.concatenate(parts, axis=1))
    ordered = dot(jnp.concatenate(pieces, axis=0).astype(BF16), order_ref[...])
    prior = ordered[:COLS] + ordered[COLS : 2 * COLS] + ordered[2 * COLS :]

    def bit_set(bit):
        return ((start_rows_ref[...] >> bit) & 1) == 1

    def band_apply(field):
        value = wide_lines(jnp.concatenate([field, field], axis=0))
        value = left(value, -15)
        for bit in range(BAND_BITS):
            value = jnp.where(bit_set(bit), left(value, 1 << bit), value)
        total = jnp.zeros((both, LINES), F32)
        for k in range(TAPS):
            total = total + weight_ref[k] * left(value, k)[:, :LINES]
        return total

    def band_adjoint(values):
        total = jnp.zeros((both, SPAN), F32)
        for k in range(TAPS):
            total = total + left(wide_lines(weight_ref[k] * values), -k)
        for bit in range(BAND_BITS):
            total = jnp.where(bit_set(bit), left(total, -(1 << bit)), total)
        total = left(total, 15)
        return (total[:COLS] + total[COLS:])[:, :LINES]

    def spectra(moved, p):
        image = maps3_ref[...] * moved[p * COLS : (p + 1) * COLS][:, None, :]
        return dot(image.reshape(COLS * COILS, LINES).astype(BF16), forward[p])

    def combine(back):
        return jnp.sum(back.reshape(COLS, COILS, LINES) * maps3_ref[...], axis=1)

    def through(field):
        moved = band_apply(field)
        return [dot(spectra(moved, p).astype(BF16), table_ref[...]) for p in range(2)]

    back = through(prior)
    residue = band_adjoint(jnp.concatenate([combine(data_ref[p] - back[p]) for p in range(2)], axis=0))
    back = through(residue)
    first = band_adjoint(jnp.concatenate([combine(back[p]) for p in range(2)], axis=0))

    moved = band_apply(first)
    squares = jnp.zeros((1, LINES), F32)
    for p in range(2):
        here = spectra(moved, p)
        squares = squares + jnp.sum(here * here.astype(BF16).astype(F32), axis=0, keepdims=True)

    def total(values):
        return jnp.sum(jnp.sum(values, axis=0, keepdims=True), axis=1, keepdims=True)

    lane1 = lane_iota(1, 128)
    sums = jnp.zeros((1, 128), F32)
    for i, part in enumerate((residue * residue, residue * first, first * first, squares)):
        sums = jnp.where(lane1 == i, total(part), sums)
    in_plane_at = x_at * 8 + lax.rem(me, 8)
    near_sum[in_plane_at] = sums

    def to_device(ref, slot, sems, device):
        pltpu.make_async_remote_copy(
            src_ref=ref.at[slot], dst_ref=ref.at[slot], send_sem=sems.at[0], recv_sem=sems.at[1],
            device_id=device, device_id_type=MESH,
        ).start()

    for at in plane:
        to_device(near_sum, in_plane_at, near_sem, in_plane(*at))

    fields = jnp.concatenate([residue, first, jnp.zeros((128 - 2 * COLS, LINES), F32)], axis=0)
    high = fields.astype(BF16)
    low = (fields - high.astype(F32)).astype(BF16)
    across = (((1,), (1,)), ((), ()))
    placed = lax.dot_general(spread_ref[...], high, across, preferred_element_type=F32)
    placed = placed + lax.dot_general(spread_ref[...], low, across, preferred_element_type=F32)
    lane = lane_iota(WIDE, 128)
    for row in range(DENSE):
        packed = jnp.zeros((WIDE, 128), F32)
        for i in range(PLACES):
            begin = 48 * i - 128 * row
            if begin < 128 and begin + 48 > 0:
                turned = placed[i * WIDE : (i + 1) * WIDE]
                if begin % 128:
                    turned = pltpu.roll(turned, begin % 128, 1)
                packed = jnp.where((lane >= begin) & (lane < begin + 48), turned, packed)
        send_fields[:, row, :] = packed

    @pl.loop(0, WIDE - 1)
    def _(k):
        to_wide(far_first(k), lambda to: send_fields.at[to], got_fields.at[me], field_sem)

    got_fields[me] = send_fields[me]

    for edge in edges:
        edge.wait()
    below = jnp.where(me > 0, 1.0, 0.0).astype(F32)
    above = jnp.where(me < WIDE - 1, 1.0, 0.0).astype(F32)
    cells = []
    for s in range(SLICES):
        rows = [edge_ref[0, i, s : s + 1, :] * below for i in range(EDGE)]
        rows += [prior_ref[i, s : s + 1, :] for i in range(ROWS)]
        rows += [edge_ref[1, i, s : s + 1, :] * above for i in range(EDGE)]
        rows += [jnp.zeros((16 - PLACES, READOUT), F32)]
        cells.append(jnp.concatenate(rows, axis=0))

    finish(near_sum, near_sum, near_sem, PLANE - 1)
    far_sum[z_at] = jnp.sum(near_sum[...].reshape(PLANE, 128), axis=0, keepdims=True)
    for at in line:
        to_device(far_sum, z_at, far_sem, in_line(at))
    finish(far_sum, far_sum, far_sem, LINE - 1)
    sums = jnp.sum(far_sum[...].reshape(LINE, 128), axis=0, keepdims=True)
    picked = [jnp.sum(jnp.where(lane1 == i, sums, 0.0), axis=1, keepdims=True) for i in range(4)]
    c0, c1 = step_scalars(*picked)
    solution_ref[...] = prior + c0 * residue + c1 * first

    finish(send_fields, got_fields, field_sem, WIDE - 1)
    lines = [got_fields[:, row, :] for row in range(DENSE)]
    pairs = []
    for m in range(6):
        begin = 96 * m
        row, off = begin // 128, begin % 128
        pair = pltpu.roll(lines[row], 128 - off, 1) if off else lines[row]
        if off + 96 > 128:
            pair = jnp.where(lane < 128 - off, pair, pltpu.roll(lines[row + 1], 128 - off, 1))
        pairs.append(pair)
    pairs = jnp.concatenate(pairs, axis=0)
    joined = c0 * pairs + c1 * pltpu.roll(pairs, 128 - COLS, 1)
    high = joined.astype(BF16)
    low = (joined - high.astype(F32)).astype(BF16)
    block_of = lax.broadcasted_iota(jnp.int32, (16, 2 * READOUT), 0)
    readout_of = lax.rem(lane_iota(16, 2 * READOUT), READOUT)
    inside = (readout_of >= COLS * block_of) & (readout_of < COLS * block_of + COLS)
    change = jnp.zeros((SLICES * 16, READOUT), F32)
    for part in (high, low):
        wide = dot(part, rep_ref[...]).reshape(6 * SLICES, 16, 2 * READOUT)
        wide = jnp.where(inside[None], wide, 0.0).reshape(6 * WIDE, 2 * READOUT).astype(BF16)
        wide = jnp.concatenate([wide[:, :READOUT], wide[:, READOUT:]], axis=0)
        change = change + dot(pick_ref[...], wide)
    cells = [cells[s] + change[16 * s : 16 * s + 16] for s in range(SLICES)]

    def diamond(near, middle, far):
        rows = jnp.concatenate([near[1:11], middle[2:10], far[3:9]], axis=0)
        return rows.astype(BF16)

    send_halo[0] = diamond(cells[3], cells[2], cells[1])
    send_halo[1] = diamond(cells[0], cells[1], cells[2])
    halos = [
        pltpu.make_async_remote_copy(
            src_ref=send_halo.at[side], dst_ref=got_halo.at[side],
            send_sem=halo_send.at[side], recv_sem=halo_recv.at[side],
            device_id={"narrow": lax.rem(nme + step, NARROW)}, device_id_type=MESH,
        )
        for side, step in ((0, 1), (1, NARROW - 1))
    ]
    for halo in halos:
        halo.start()
    for halo in halos:
        halo.wait()

    def opened(side, keep):
        rows = got_halo[side].astype(F32) * keep
        zero = jnp.zeros((8, READOUT), F32)
        near = jnp.concatenate([zero[:1], rows[:10], zero[:5]], axis=0)
        middle = jnp.concatenate([zero[:2], rows[10:18], zero[:6]], axis=0)
        far = jnp.concatenate([zero[:3], rows[18:24], zero[:7]], axis=0)
        return near, middle, far

    has_low = jnp.where(nme > 0, 1.0, 0.0).astype(F32)
    has_high = jnp.where(nme < NARROW - 1, 1.0, 0.0).astype(F32)
    near_low, mid_low, far_low = opened(0, has_low)
    near_high, mid_high, far_high = opened(1, has_high)
    volume = [far_low, mid_low, near_low] + cells + [near_high, mid_high, far_high]
    keeps = [has_low] * 3 + [None] * SLICES + [has_high] * 3
    margin = jnp.zeros((16, 128), F32)
    volume = [jnp.concatenate([one, margin], axis=1) for one in volume]
    line_of = lax.broadcasted_iota(jnp.int32, (16, READOUT + 128), 0) + (ROWS * me - EDGE)
    in_grid = (line_of >= 0) & (line_of < LINES) & (lane_iota(16, READOUT + 128) < READOUT)
    in_grid = in_grid.astype(F32)

    def flux(jump):
        return jump / (1.0 + jump * jump)

    for step in range(DIFF_STEPS):
        last = len(volume) - 1
        across_slices = [flux(volume[i + 1] - volume[i]) for i in range(last)]
        after = []
        for i in range(1, last):
            one = volume[i]
            down = flux(pltpu.roll(one, 15, 0) - one)
            along = flux(pltpu.roll(one, SPAN - 1, 1) - one)
            moved = axis_weights[0] * (down - pltpu.roll(down, 1, 0))
            moved = moved + axis_weights[1] * (across_slices[i] - across_slices[i - 1])
            moved = moved + axis_weights[2] * (along - pltpu.roll(along, 1, 1))
            grid = in_grid if keeps[i] is None else in_grid * keeps[i]
            after.append((one + time_step * moved) * grid)
        volume = after
        keeps = keeps[1:-1]
    for s in range(SLICES):
        for i in range(ROWS):
            denoised_ref[i, s : s + 1, :] = volume[s][EDGE + i : EDGE + i + 1, :READOUT]


def whole(prior, coil_maps, kspace, band_start, frac, mask):
    vmem = pl.BlockSpec(memory_space=pltpu.VMEM)
    far = pl.BlockSpec(memory_space=pltpu.HBM)
    table = cosine_table()
    constants = (table, table.T) + place_tables() + return_tables()
    constants = [jnp.asarray(one, BF16) for one in constants]
    moved = [kspace, frac] + constants + [prior, coil_maps, band_start]
    return pl.pallas_call(
        whole_body,
        out_shape=(
            jax.ShapeDtypeStruct((COLS, LINES), F32),
            jax.ShapeDtypeStruct((ROWS, SLICES, READOUT), F32),
        ),
        in_specs=[far] * (len(moved) + 1),
        out_specs=(vmem, vmem),
        scratch_shapes=[pltpu.SMEM(mask.shape, mask.dtype)]
        + [pltpu.VMEM(one.shape, one.dtype) for one in moved]
        + [
            pltpu.VMEM((WIDE, 8, LINES), BF16),
            pltpu.VMEM((WIDE, 8, LINES), BF16),
            pltpu.VMEM((2, EDGE, SLICES, READOUT), F32),
            pltpu.VMEM((COLS, COILS, LINES), F32),
            pltpu.VMEM((TAPS, 2 * COLS, LINES), F32),
            pltpu.VMEM((2, COLS * COILS, LINES), F32),
            pltpu.VMEM((2 * COLS, SPAN), jnp.int32),
            pltpu.VMEM((WIDE, DENSE, 128), F32),
            pltpu.VMEM((WIDE, DENSE, 128), F32),
            pltpu.VMEM((PLANE, 1, 128), F32),
            pltpu.VMEM((LINE, 1, 128), F32),
            pltpu.VMEM((2, HALO, READOUT), BF16),
            pltpu.VMEM((2, HALO, READOUT), BF16),
            pltpu.SemaphoreType.DMA((len(moved) + 1,)),
            pltpu.SemaphoreType.DMA((2,)),
            pltpu.SemaphoreType.DMA((2,)),
            pltpu.SemaphoreType.DMA((2,)),
            pltpu.SemaphoreType.DMA((2,)),
            pltpu.SemaphoreType.DMA((2,)),
            pltpu.SemaphoreType.DMA((2,)),
            pltpu.SemaphoreType.DMA((2,)),
            pltpu.SemaphoreType.DMA((2,)),
        ],
        compiler_params=pltpu.CompilerParams(collective_id=0, has_side_effects=True, vmem_limit_bytes=63 << 20),
        name="whole",
    )(mask, *moved)


def per_device(prior, coil_maps, kspace, band_start, band_frac, shot_mask):
    solved, denoised = whole(
        prior, coil_maps, kspace, band_start, jnp.transpose(band_frac, (0, 2, 1)), jnp.transpose(shot_mask, (0, 2, 1))
    )
    return jnp.transpose(solved), denoised


def solution(mesh):
    in_specs = (
        P("wide", "narrow", None),
        P("wide", "narrow"),
        P(None, None, ("narrow", "wide")),
        P(None, ("narrow", "wide")),
        P(None, None, ("narrow", "wide")),
        P(None, None, "narrow"),
    )
    out_specs = (P(None, ("narrow", "wide")), P("wide", "narrow", None))
    return jax.shard_map(per_device, mesh=mesh, in_specs=in_specs, out_specs=out_specs, check_vma=False)
```

```python
import functools
import math

import jax
import jax.numpy as jnp
import numpy as np
from jax import lax
from jax.experimental import pallas as pl
from jax.experimental.pallas import tpu as pltpu
from jax.sharding import PartitionSpec as P

SHOTS = 6
TAPS = 8
DIFF_STEPS = 3
COILS = 16
WIDE = 64
NARROW = 8
PLANE = 32
LINE = 16
LINES = 384
COLS = 24
ROWS = 6
SLICES = 4
READOUT = 384
SPAN = 512
PIECES = 3
EDGE = DIFF_STEPS
PLACES = ROWS + 2 * EDGE
PLACE_ROWS = (3, 4, 5, 6, 7, 8, 2, 9, 1, 10, 0, 11)
DENSE = 5
HALO = 24
BAND_BITS = 5

penalty = 0.5
time_step = 0.18
axis_weights = (1.0, 0.5, 1.0)

F32 = jnp.float32
BF16 = jnp.bfloat16
MESH = pl.DeviceIdType.MESH


def cosine_table():
    freq = np.arange(LINES, dtype=np.float32)[:, None]
    cell = np.arange(LINES, dtype=np.float32)[None, :]
    angle = np.float32(math.pi) * (cell + np.float32(0.5)) * freq / np.float32(LINES)
    entries = np.cos(angle).astype(np.float32) * np.float32(math.sqrt(2.0 / LINES))
    entries = entries * np.where(freq == 0.0, np.float32(math.sqrt(0.5)), np.float32(1.0))
    return entries.astype(np.float32)


def place_tables():
    place = np.zeros((WIDE * 8, LINES + 128), np.float32)
    for w in range(WIDE):
        for i in range(ROWS):
            place[8 * w + i, ROWS * w + i] = 1.0
        for g in range(2):
            place[8 * w + 6 + g, LINES + g * 64 + w] = 1.0
    order = np.zeros((3 * 128, LINES), np.float32)
    for t in range(3):
        for g in range(2):
            for w in range(WIDE):
                order[t * 128 + g * 64 + w, ROWS * w + 3 * g + t] = 1.0
    return place, order


def return_tables():
    spread = np.zeros((PLACES * WIDE, LINES), np.float32)
    for i in range(PLACES):
        for w in range(WIDE):
            line = ROWS * w - EDGE + PLACE_ROWS[i]
            if 0 <= line < LINES:
                spread[i * WIDE + w, line] = 1.0
    rep = np.zeros((128, 2 * READOUT), np.float32)
    for i in range(2):
        for x in range(READOUT):
            rep[48 * i + x % COLS, i * READOUT + x] = 1.0
    pick = np.zeros((SLICES * 16, 2 * 6 * WIDE), np.float32)
    for i in range(2):
        for m in range(6):
            for w in range(WIDE):
                pick[(w // 16) * 16 + PLACE_ROWS[2 * m + i], (i * 6 + m) * WIDE + w] = 1.0
    return spread, rep, pick


def lane_iota(rows, lanes):
    return lax.broadcasted_iota(jnp.int32, (rows, lanes), 1)


def poly_sin(x):
    x2 = x * x
    return x * (1.0 + x2 * (-1.0 / 6 + x2 * (1.0 / 120 + x2 * (-1.0 / 5040 + x2 * (1.0 / 362880)))))


def poly_cos(x):
    x2 = x * x
    return 1.0 + x2 * (-0.5 + x2 * (1.0 / 24 + x2 * (-1.0 / 720 + x2 * (1.0 / 40320 - x2 * (1.0 / 3628800)))))


def tap_weights(frac):
    near = jnp.minimum(frac, 1.0 - frac) * (math.pi / 2)
    full = 2.0 * poly_sin(near) * poly_cos(near)
    phi = frac * (math.pi / 4)
    sin_a, cos_a = poly_sin(phi), poly_cos(phi)
    rest = (1.0 - frac) * (math.pi / 4)
    sin_b, cos_b = poly_sin(rest), poly_cos(rest)
    quarter = {-3: -sin_b, -2: -cos_a, -1: -cos_b, 0: -sin_a, 1: sin_b, 2: cos_a, 3: cos_b, 4: sin_a}
    weights = []
    for k in range(TAPS):
        n = k - 3
        t = n - frac
        sign = 1.0 if n % 2 else -1.0
        if n in (0, 1):
            small = jnp.abs(t) < 1e-5
            inverse = 1.0 / jnp.where(small, 1.0, t)
            product = (full * inverse) * (quarter[n] * inverse) * (sign * 4.0 / math.pi**2)
            weights.append(jnp.where(small, 1.0, product))
        else:
            inverse = 1.0 / t
            weights.append((full * inverse) * (quarter[n] * inverse) * (sign * 4.0 / math.pi**2))
    return weights


def wide_lines(values):
    return jnp.concatenate([values, jnp.zeros((values.shape[0], SPAN - LINES), F32)], axis=1)


def left(values, count):
    return pltpu.roll(values, (SPAN - count) % SPAN, 1) if count % SPAN else values


def split3(values):
    high = values.astype(BF16)
    rest = values - high.astype(F32)
    middle = rest.astype(BF16)
    low = (rest - middle.astype(F32)).astype(BF16)
    return high, middle, low


def dot(a, b):
    return jnp.dot(a, b, preferred_element_type=F32)


def dot_first(a, b):
    return lax.dot_general(a, b, (((0,), (0,)), ((), ())), preferred_element_type=F32)


def step_scalars(rr, ra, aa, ab):
    alpha = rr / (penalty * rr + ra)
    rho = ra / rr
    qq = jnp.maximum(aa - rho * ra, 0.0)
    qaq = ab - 2.0 * rho * aa + rho * rho * ra
    next_rr = alpha * alpha * qq
    beta = next_rr / rr
    direction_sq = next_rr + beta * beta * rr
    direction_a = alpha * alpha * qaq - 2.0 * beta * alpha * qq + beta * beta * ra
    image = jnp.maximum(penalty * direction_sq + direction_a, penalty * direction_sq)
    second = jnp.where(image > 0.0, next_rr / jnp.where(image > 0.0, image, 1.0), 0.0)
    return alpha + second * (alpha * rho + beta), -second * alpha


def whole_body(
    mask_any, kspace_any, frac_any, table_any, turned_any, place_any, order_any,
    spread_any, rep_any, pick_any, prior_any, maps_any, start_any,
    solution_ref, denoised_ref,
    mask_ref, kspace_ref, frac_ref, table_ref, turned_ref, place_ref, order_ref, spread_ref, rep_ref, pick_ref,
    prior_ref, maps_ref, start_ref,
    send_maps, got_ref, edge_ref, maps3_ref, weight_ref, data_ref, start_rows_ref,
    send_fields, got_fields, near_sum, far_sum, send_halo, got_halo, got_cross, send_dia, got_dia,
    load_sem, maps_sem, edge_send, edge_recv, field_sem, near_sem, far_sem, halo_send, halo_recv,
    cross_sem, near_cross, dia_sem,
):
    me = lax.axis_index("wide")
    nme = lax.axis_index("narrow")
    my_slice = me // 16
    both = 2 * COLS
    z_lo = me // 8
    got_halo[...] = jnp.zeros(got_halo.shape, BF16)
    got_cross[...] = jnp.zeros(got_cross.shape, F32)
    got_dia[...] = jnp.zeros(got_dia.shape, F32)
    barrier = pltpu.get_barrier_semaphore()

    def far_first(k):
        step = k // 8
        half = lax.rem(z_lo // 4 + 1 - step // 4 + 2, 2)
        return (4 * half + lax.rem(z_lo + 7 - step, 4)) * 8 + lax.rem(me + 7 - lax.rem(k, 8), 8)

    sources = (
        kspace_any, frac_any, table_any, turned_any, place_any, order_any, spread_any, rep_any, pick_any,
        prior_any, maps_any, start_any, mask_any,
    )
    targets = (
        kspace_ref, frac_ref, table_ref, turned_ref, place_ref, order_ref, spread_ref, rep_ref, pick_ref,
        prior_ref, maps_ref, start_ref, mask_ref,
    )
    loads = [pltpu.make_async_copy(a, b, load_sem.at[i]) for i, (a, b) in enumerate(zip(sources, targets))]
    for i in (9, 10, 11, 12, 1, 3, 0, 2, 4, 5, 6, 7, 8):
        loads[i].start()

    core, y_at = lax.rem(me, 2), lax.rem(me // 2, 4)
    x_at, z_hi = lax.rem(nme, 4), nme // 4
    z_at = z_hi * 8 + z_lo
    middle_pair = (nme == 3) | (nme == 4)
    across_to = NARROW - 1 - nme
    distance = jnp.where(nme == 3, SLICES - my_slice, my_slice + 1)
    crosses = middle_pair & (distance <= EDGE)

    def in_plane(a, b, c):
        wide_to = z_lo * 8 + lax.rem(y_at + b, 4) * 2 + lax.rem(core + c, 2)
        return {"wide": wide_to, "narrow": z_hi * 4 + lax.rem(x_at + a, 4)}

    def in_line(a):
        z_to = lax.rem(z_at + a, 16)
        return {"wide": lax.rem(z_to, 8) * 8 + lax.rem(me, 8), "narrow": (z_to // 8) * 4 + x_at}

    plane = [(a, b, c) for a in range(4) for b in range(4) for c in range(2) if (a, b, c) != (0, 0, 0)]
    plane.sort(key=lambda at: -(min(at[0], 4 - at[0]) + min(at[1], 4 - at[1])))
    line = sorted(range(1, 16), key=lambda a: -min(a, 16 - a))

    @pl.loop(1, 8)
    def _(k):
        other = {"wide": lax.rem(me + 8 * k, WIDE), "narrow": (1 - z_hi) * 4 + x_at}
        pl.semaphore_signal(barrier, inc=1, device_id=other, device_id_type=MESH)

    @pl.loop(1, NARROW)
    def _(k):
        pl.semaphore_signal(barrier, inc=1, device_id={"narrow": lax.rem(nme + k, NARROW)}, device_id_type=MESH)

    @pl.loop(0, WIDE - 1, unroll=9)
    def _(k):
        pl.semaphore_signal(barrier, inc=1, device_id={"wide": far_first(k)}, device_id_type=MESH)

    for a, b, c in plane:
        if a and (b or c):
            pl.semaphore_signal(barrier, inc=1, device_id=in_plane(a, b, c), device_id_type=MESH)

    loads[9].wait()
    loads[10].wait()
    lane8 = lane_iota(8, 128)
    stacked = [jnp.concatenate([prior_ref[t], prior_ref[3 + t]], axis=0) for t in range(3)]
    for q in range(16):
        packed = jnp.zeros((8, 128), F32)
        for t in range(3):
            turned = pltpu.roll(stacked[t], (24 * t - 24 * q) % READOUT, 1)[:, :128]
            packed = jnp.where((lane8 >= 24 * t) & (lane8 < 24 * t + 24), turned, packed)
        high = packed.astype(BF16).astype(F32)
        rest = packed - high
        middle = rest.astype(BF16).astype(F32)
        low = rest - middle
        packed = jnp.concatenate([high, middle, low], axis=1)
        for s in range(SLICES):
            d = 16 * s + q
            block = maps_ref[:, d * 384 : (d + 1) * 384].astype(F32)
            message = jnp.concatenate([block, packed[s : s + 1], packed[4 + s : 5 + s]], axis=0)
            send_maps[d] = message.astype(BF16)

    pl.semaphore_wait(barrier, WIDE + NARROW - 2 + 21 + 7)

    def to_wide(to, source, target, sems):
        pltpu.make_async_remote_copy(
            src_ref=source(to), dst_ref=target, send_sem=sems.at[0], recv_sem=sems.at[1],
            device_id={"wide": to}, device_id_type=MESH,
        ).start()

    def finish(source, target, sems, count):
        others = pl.ds(0, count)
        pltpu.make_async_copy(source.at[others], source.at[others], sems.at[0]).wait()
        pltpu.make_async_copy(target.at[others], target.at[others], sems.at[1]).wait()

    @pl.loop(1, WIDE, unroll=9)
    def _(k):
        to_wide(lax.rem(me + k, WIDE), lambda to: send_maps.at[to], got_ref.at[me], maps_sem)

    got_ref[me] = send_maps[me]

    edges = [
        pltpu.make_async_remote_copy(
            src_ref=prior_ref.at[pl.ds(first, EDGE)], dst_ref=edge_ref.at[side],
            send_sem=edge_send.at[side], recv_sem=edge_recv.at[side],
            device_id={"wide": lax.rem(me + step, WIDE)}, device_id_type=MESH,
        )
        for side, first, step in ((0, ROWS - EDGE, 1), (1, 0, WIDE - 1))
    ]
    for edge in edges:
        edge.start()

    loads[11].wait()
    loads[12].wait()
    starts = []
    diagonal = lax.broadcasted_iota(jnp.int32, (COLS, COLS), 0) == lax.broadcasted_iota(jnp.int32, (COLS, COLS), 1)
    for p in range(2):
        row = jnp.broadcast_to(start_ref[p : p + 1, :].astype(F32), (COLS, COLS))
        starts.append(jnp.sum(jnp.where(diagonal, row, 0.0), axis=1, keepdims=True))
    ahead = jnp.concatenate(starts, axis=0).astype(jnp.int32) + 12
    start_rows_ref[...] = jnp.broadcast_to(ahead, (both, SPAN))

    loads[1].wait()
    frac = jnp.concatenate([frac_ref[0], frac_ref[1]], axis=0)
    for k, weight in enumerate(tap_weights(frac)):
        weight_ref[k] = weight

    shot = lax.rem(lane_iota(1, LINES), SHOTS)
    masks = []
    for p in range(2):
        row = jnp.zeros((1, LINES), F32)
        for h in range(SHOTS):
            row = jnp.where(shot == h, mask_ref[p, my_slice, h].astype(F32), row)
        masks.append(row)
    loads[3].wait()
    turned = turned_ref[...].astype(F32)
    forward = [(turned * masks[p]).astype(BF16) for p in range(2)]
    loads[0].wait()
    for p in range(2):
        data_ref[p] = lax.dot_general(
            kspace_ref[p], forward[p], (((0,), (1,)), ((), ())), preferred_element_type=F32
        )
    for i in (2, 4, 5, 6, 7, 8):
        loads[i].wait()

    finish(send_maps, got_ref, maps_sem, WIDE - 1)
    got = got_ref[...].reshape(WIDE * 8, LINES)
    laid = dot_first(got, place_ref[...])
    maps3_ref[...] = laid[:, :LINES].reshape(COLS, COILS, LINES)
    pieces = []
    for m in range(PIECES):
        parts = [laid[m * 128 + 24 * t : m * 128 + 24 * t + 24, LINES:] for t in range(3)]
        pieces.append(jnp.concatenate(parts, axis=1))
    ordered = dot(jnp.concatenate(pieces, axis=0).astype(BF16), order_ref[...])
    prior = ordered[:COLS] + ordered[COLS : 2 * COLS] + ordered[2 * COLS :]

    def bit_set(bit):
        return ((start_rows_ref[...] >> bit) & 1) == 1

    def band_apply(field):
        value = wide_lines(jnp.concatenate([field, field], axis=0))
        value = left(value, -15)
        for bit in range(BAND_BITS):
            value = jnp.where(bit_set(bit), left(value, 1 << bit), value)
        total = jnp.zeros((both, LINES), F32)
        for k in range(TAPS):
            total = total + weight_ref[k] * left(value, k)[:, :LINES]
        return total

    def band_adjoint(values):
        total = jnp.zeros((both, SPAN), F32)
        for k in range(TAPS):
            total = total + left(wide_lines(weight_ref[k] * values), -k)
        for bit in range(BAND_BITS):
            total = jnp.where(bit_set(bit), left(total, -(1 << bit)), total)
        total = left(total, 15)
        return (total[:COLS] + total[COLS:])[:, :LINES]

    def spectra(moved, p):
        image = maps3_ref[...] * moved[p * COLS : (p + 1) * COLS][:, None, :]
        return dot(image.reshape(COLS * COILS, LINES).astype(BF16), forward[p])

    def combine(back):
        return jnp.sum(back.reshape(COLS, COILS, LINES) * maps3_ref[...], axis=1)

    def through(field):
        moved = band_apply(field)
        return [dot(spectra(moved, p).astype(BF16), table_ref[...]) for p in range(2)]

    back = through(prior)
    residue = band_adjoint(jnp.concatenate([combine(data_ref[p] - back[p]) for p in range(2)], axis=0))
    back = through(residue)
    first = band_adjoint(jnp.concatenate([combine(back[p]) for p in range(2)], axis=0))

    moved = band_apply(first)
    squares = jnp.zeros((1, LINES), F32)
    for p in range(2):
        here = spectra(moved, p)
        squares = squares + jnp.sum(here * here.astype(BF16).astype(F32), axis=0, keepdims=True)

    def total(values):
        return jnp.sum(jnp.sum(values, axis=0, keepdims=True), axis=1, keepdims=True)

    lane1 = lane_iota(1, 128)
    sums = jnp.zeros((1, 128), F32)
    for i, part in enumerate((residue * residue, residue * first, first * first, squares)):
        sums = jnp.where(lane1 == i, total(part), sums)
    in_plane_at = x_at * 8 + lax.rem(me, 8)
    near_sum[in_plane_at] = sums

    def to_device(ref, slot, sems, device):
        pltpu.make_async_remote_copy(
            src_ref=ref.at[slot], dst_ref=ref.at[slot], send_sem=sems.at[0], recv_sem=sems.at[1],
            device_id=device, device_id_type=MESH,
        ).start()

    for at in plane:
        to_device(near_sum, in_plane_at, near_sem, in_plane(*at))

    fields = jnp.concatenate([residue, first, jnp.zeros((128 - 2 * COLS, LINES), F32)], axis=0)
    high = fields.astype(BF16)
    low = (fields - high.astype(F32)).astype(BF16)
    across = (((1,), (1,)), ((), ()))
    placed = lax.dot_general(spread_ref[...], high, across, preferred_element_type=F32)
    placed = placed + lax.dot_general(spread_ref[...], low, across, preferred_element_type=F32)
    lane = lane_iota(WIDE, 128)
    for row in range(DENSE):
        packed = jnp.zeros((WIDE, 128), F32)
        for i in range(PLACES):
            begin = 48 * i - 128 * row
            if begin < 128 and begin + 48 > 0:
                turned = placed[i * WIDE : (i + 1) * WIDE]
                if begin % 128:
                    turned = pltpu.roll(turned, begin % 128, 1)
                packed = jnp.where((lane >= begin) & (lane < begin + 48), turned, packed)
        send_fields[:, row, :] = packed

    @pl.loop(0, WIDE - 1, unroll=9)
    def _(k):
        to_wide(far_first(k), lambda to: send_fields.at[to], got_fields.at[me], field_sem)

    got_fields[me] = send_fields[me]

    for edge in edges:
        edge.wait()
    below = jnp.where(me > 0, 1.0, 0.0).astype(F32)
    above = jnp.where(me < WIDE - 1, 1.0, 0.0).astype(F32)
    cells = []
    for s in range(SLICES):
        rows = [edge_ref[0, i, s : s + 1, :] * below for i in range(EDGE)]
        rows += [prior_ref[i, s : s + 1, :] for i in range(ROWS)]
        rows += [edge_ref[1, i, s : s + 1, :] * above for i in range(EDGE)]
        rows += [jnp.zeros((16 - PLACES, READOUT), F32)]
        cells.append(jnp.concatenate(rows, axis=0))

    def diamond(near, middle, far):
        return jnp.concatenate([near[1:11], middle[2:10], far[3:9]], axis=0)

    send_dia[...] = jnp.where(nme == 3, diamond(cells[3], cells[2], cells[1]), diamond(cells[0], cells[1], cells[2]))
    dia = pltpu.make_async_remote_copy(
        src_ref=send_dia, dst_ref=got_dia, send_sem=dia_sem.at[0], recv_sem=dia_sem.at[1],
        device_id={"narrow": across_to}, device_id_type=MESH,
    )

    @pl.when(middle_pair)
    def _():
        dia.start()

    finish(near_sum, near_sum, near_sem, PLANE - 1)
    far_sum[z_at] = jnp.sum(near_sum[...].reshape(PLANE, 128), axis=0, keepdims=True)
    for at in line:
        to_device(far_sum, z_at, far_sem, in_line(at))

    def cross(rows, sems):
        @pl.loop(0, WIDE, unroll=8)
        def _(k):
            step = k // 8
            ahead_by = jnp.where(lax.rem(step, 2) == 1, (step + 1) // 2, 8 - step // 2)
            to = lax.rem(z_lo + ahead_by, 8) * 8 + lax.rem(me + 4 + k, 8)
            pltpu.make_async_remote_copy(
                src_ref=send_fields.at[to, pl.ds(0, rows)], dst_ref=got_cross.at[me, pl.ds(0, rows)],
                send_sem=sems.at[0], recv_sem=sems.at[1],
                device_id={"wide": to, "narrow": across_to}, device_id_type=MESH,
            ).start()

    @pl.when(crosses & (distance == 1))
    def _():
        cross(4, near_cross)

    @pl.when(crosses & (distance > 1))
    def _():
        cross(3, cross_sem)

    finish(far_sum, far_sum, far_sem, LINE - 1)
    sums = jnp.sum(far_sum[...].reshape(LINE, 128), axis=0, keepdims=True)
    picked = [jnp.sum(jnp.where(lane1 == i, sums, 0.0), axis=1, keepdims=True) for i in range(4)]
    c0, c1 = step_scalars(*picked)
    solution_ref[...] = prior + c0 * residue + c1 * first

    finish(send_fields, got_fields, field_sem, WIDE - 1)
    def unpack(source):
        lines = [source[:, row, :] for row in range(DENSE)]
        pairs = []
        for m in range(6):
            begin = 96 * m
            row, off = begin // 128, begin % 128
            pair = pltpu.roll(lines[row], 128 - off, 1) if off else lines[row]
            if off + 96 > 128:
                pair = jnp.where(lane < 128 - off, pair, pltpu.roll(lines[row + 1], 128 - off, 1))
            pairs.append(pair)
        pairs = jnp.concatenate(pairs, axis=0)
        joined = c0 * pairs + c1 * pltpu.roll(pairs, 128 - COLS, 1)
        high = joined.astype(BF16)
        low = (joined - high.astype(F32)).astype(BF16)
        block_of = lax.broadcasted_iota(jnp.int32, (16, 2 * READOUT), 0)
        readout_of = lax.rem(lane_iota(16, 2 * READOUT), READOUT)
        inside = (readout_of >= COLS * block_of) & (readout_of < COLS * block_of + COLS)
        change = jnp.zeros((SLICES * 16, READOUT), F32)
        for part in (high, low):
            wide = dot(part, rep_ref[...]).reshape(6 * SLICES, 16, 2 * READOUT)
            wide = jnp.where(inside[None], wide, 0.0).reshape(6 * WIDE, 2 * READOUT).astype(BF16)
            wide = jnp.concatenate([wide[:, :READOUT], wide[:, READOUT:]], axis=0)
            change = change + dot(pick_ref[...], wide)
        return [change[16 * s : 16 * s + 16] for s in range(SLICES)]

    change = unpack(got_fields)
    cells = [cells[s] + change[s] for s in range(SLICES)]

    send_halo[0] = diamond(cells[3], cells[2], cells[1]).astype(BF16)
    send_halo[1] = diamond(cells[0], cells[1], cells[2]).astype(BF16)
    up, down = (
        pltpu.make_async_remote_copy(
            src_ref=send_halo.at[side], dst_ref=got_halo.at[side],
            send_sem=halo_send.at[side], recv_sem=halo_recv.at[side],
            device_id={"narrow": lax.rem(nme + step, NARROW)}, device_id_type=MESH,
        )
        for side, step in ((0, 1), (1, NARROW - 1))
    )

    @pl.when(x_at < 3)
    def _():
        up.start()

    @pl.when(x_at > 0)
    def _():
        down.start()

    def wait_cross(ref, count, rows, sem):
        part = ref.at[pl.ds(0, count), pl.ds(0, rows)]
        pltpu.make_async_copy(part, part, sem).wait()

    @pl.when(crosses & (distance == 1))
    def _():
        wait_cross(send_fields, WIDE, 4, near_cross.at[0])

    @pl.when(crosses & (distance > 1))
    def _():
        wait_cross(send_fields, WIDE, 3, cross_sem.at[0])

    @pl.when(middle_pair)
    def _():
        dia.wait()
        wait_cross(got_cross, 16, 4, near_cross.at[1])
        wait_cross(got_cross, 32, 3, cross_sem.at[1])

    crossed = unpack(got_cross)
    crossed = jnp.where(
        nme == 3, diamond(crossed[0], crossed[1], crossed[2]), diamond(crossed[3], crossed[2], crossed[1])
    )
    crossed = crossed + got_dia[...]

    @pl.when(x_at < 3)
    def _():
        up.wait_send()
        down.wait_recv()

    @pl.when(x_at > 0)
    def _():
        down.wait_send()
        up.wait_recv()

    def opened(rows):
        zero = jnp.zeros((8, READOUT), F32)
        near = jnp.concatenate([zero[:1], rows[:10], zero[:5]], axis=0)
        middle = jnp.concatenate([zero[:2], rows[10:18], zero[:6]], axis=0)
        far = jnp.concatenate([zero[:3], rows[18:24], zero[:7]], axis=0)
        return near, middle, far

    has_low = jnp.where(nme > 0, 1.0, 0.0).astype(F32)
    has_high = jnp.where(nme < NARROW - 1, 1.0, 0.0).astype(F32)
    near_low, mid_low, far_low = opened(jnp.where(nme == 4, crossed, got_halo[0].astype(F32)))
    near_high, mid_high, far_high = opened(jnp.where(nme == 3, crossed, got_halo[1].astype(F32)))
    volume = [far_low, mid_low, near_low] + cells + [near_high, mid_high, far_high]
    keeps = [has_low] * 3 + [None] * SLICES + [has_high] * 3
    margin = jnp.zeros((16, 128), F32)
    volume = [jnp.concatenate([one, margin], axis=1) for one in volume]
    line_of = lax.broadcasted_iota(jnp.int32, (16, READOUT + 128), 0) + (ROWS * me - EDGE)
    in_grid = (line_of >= 0) & (line_of < LINES) & (lane_iota(16, READOUT + 128) < READOUT)
    in_grid = in_grid.astype(F32)

    def flux(jump):
        return jump / (1.0 + jump * jump)

    for step in range(DIFF_STEPS):
        last = len(volume) - 1
        across_slices = [flux(volume[i + 1] - volume[i]) for i in range(last)]
        after = []
        for i in range(1, last):
            one = volume[i]
            down = flux(pltpu.roll(one, 15, 0) - one)
            along = flux(pltpu.roll(one, SPAN - 1, 1) - one)
            moved = axis_weights[0] * (down - pltpu.roll(down, 1, 0))
            moved = moved + axis_weights[1] * (across_slices[i] - across_slices[i - 1])
            moved = moved + axis_weights[2] * (along - pltpu.roll(along, 1, 1))
            grid = in_grid if keeps[i] is None else in_grid * keeps[i]
            after.append((one + time_step * moved) * grid)
        volume = after
        keeps = keeps[1:-1]
    for s in range(SLICES):
        for i in range(ROWS):
            denoised_ref[i, s : s + 1, :] = volume[s][EDGE + i : EDGE + i + 1, :READOUT]


def whole(prior, coil_maps, kspace, band_start, frac, mask):
    vmem = pl.BlockSpec(memory_space=pltpu.VMEM)
    far = pl.BlockSpec(memory_space=pltpu.HBM)
    table = cosine_table()
    constants = (table, table.T) + place_tables() + return_tables()
    constants = [jnp.asarray(one, BF16) for one in constants]
    moved = [kspace, frac] + constants + [prior, coil_maps, band_start]
    return pl.pallas_call(
        whole_body,
        out_shape=(
            jax.ShapeDtypeStruct((COLS, LINES), F32),
            jax.ShapeDtypeStruct((ROWS, SLICES, READOUT), F32),
        ),
        in_specs=[far] * (len(moved) + 1),
        out_specs=(vmem, vmem),
        scratch_shapes=[pltpu.SMEM(mask.shape, mask.dtype)]
        + [pltpu.VMEM(one.shape, one.dtype) for one in moved]
        + [
            pltpu.VMEM((WIDE, 8, LINES), BF16),
            pltpu.VMEM((WIDE, 8, LINES), BF16),
            pltpu.VMEM((2, EDGE, SLICES, READOUT), F32),
            pltpu.VMEM((COLS, COILS, LINES), F32),
            pltpu.VMEM((TAPS, 2 * COLS, LINES), F32),
            pltpu.VMEM((2, COLS * COILS, LINES), F32),
            pltpu.VMEM((2 * COLS, SPAN), jnp.int32),
            pltpu.VMEM((WIDE, DENSE, 128), F32),
            pltpu.VMEM((WIDE, DENSE, 128), F32),
            pltpu.VMEM((PLANE, 1, 128), F32),
            pltpu.VMEM((LINE, 1, 128), F32),
            pltpu.VMEM((2, HALO, READOUT), BF16),
            pltpu.VMEM((2, HALO, READOUT), BF16),
            pltpu.VMEM((WIDE, DENSE, 128), F32),
            pltpu.VMEM((HALO, READOUT), F32),
            pltpu.VMEM((HALO, READOUT), F32),
            pltpu.SemaphoreType.DMA((len(moved) + 1,)),
            pltpu.SemaphoreType.DMA((2,)),
            pltpu.SemaphoreType.DMA((2,)),
            pltpu.SemaphoreType.DMA((2,)),
            pltpu.SemaphoreType.DMA((2,)),
            pltpu.SemaphoreType.DMA((2,)),
            pltpu.SemaphoreType.DMA((2,)),
            pltpu.SemaphoreType.DMA((2,)),
            pltpu.SemaphoreType.DMA((2,)),
            pltpu.SemaphoreType.DMA((2,)),
            pltpu.SemaphoreType.DMA((2,)),
            pltpu.SemaphoreType.DMA((2,)),
        ],
        compiler_params=pltpu.CompilerParams(collective_id=0, has_side_effects=True, vmem_limit_bytes=63 << 20),
        name="whole",
    )(mask, *moved)


def per_device(prior, coil_maps, kspace, band_start, band_frac, shot_mask):
    solved, denoised = whole(
        prior, coil_maps, kspace, band_start, jnp.transpose(band_frac, (0, 2, 1)), jnp.transpose(shot_mask, (0, 2, 1))
    )
    return jnp.transpose(solved), denoised


def solution(mesh):
    in_specs = (
        P("wide", "narrow", None),
        P("wide", "narrow"),
        P(None, None, ("narrow", "wide")),
        P(None, ("narrow", "wide")),
        P(None, None, ("narrow", "wide")),
        P(None, None, "narrow"),
    )
    out_specs = (P(None, ("narrow", "wide")), P("wide", "narrow", None))
    return jax.shard_map(per_device, mesh=mesh, in_specs=in_specs, out_specs=out_specs, check_vma=False)
```

```python
import functools
import math

import jax
import jax.numpy as jnp
import numpy as np
from jax import lax
from jax.experimental import pallas as pl
from jax.experimental.pallas import tpu as pltpu
from jax.sharding import PartitionSpec as P

SHOTS = 6
TAPS = 8
DIFF_STEPS = 3
COILS = 16
WIDE = 64
NARROW = 8
PLANE = 32
LINE = 16
LINES = 384
COLS = 24
ROWS = 6
SLICES = 4
READOUT = 384
SPAN = 512
PIECES = 3
EDGE = DIFF_STEPS
PLACES = ROWS + 2 * EDGE
PLACE_ROWS = (3, 4, 5, 6, 7, 8, 2, 9, 1, 10, 0, 11)
DENSE = 5
HALO = 24
BAND_BITS = 5

penalty = 0.5
time_step = 0.18
axis_weights = (1.0, 0.5, 1.0)

F32 = jnp.float32
BF16 = jnp.bfloat16
MESH = pl.DeviceIdType.MESH


def cosine_table():
    freq = np.arange(LINES, dtype=np.float32)[:, None]
    cell = np.arange(LINES, dtype=np.float32)[None, :]
    angle = np.float32(math.pi) * (cell + np.float32(0.5)) * freq / np.float32(LINES)
    entries = np.cos(angle).astype(np.float32) * np.float32(math.sqrt(2.0 / LINES))
    entries = entries * np.where(freq == 0.0, np.float32(math.sqrt(0.5)), np.float32(1.0))
    return entries.astype(np.float32)


def place_tables():
    place = np.zeros((WIDE * 8, LINES + 128), np.float32)
    for w in range(WIDE):
        for i in range(ROWS):
            place[8 * w + i, ROWS * w + i] = 1.0
        for g in range(2):
            place[8 * w + 6 + g, LINES + g * 64 + w] = 1.0
    order = np.zeros((3 * 128, LINES), np.float32)
    for t in range(3):
        for g in range(2):
            for w in range(WIDE):
                order[t * 128 + g * 64 + w, ROWS * w + 3 * g + t] = 1.0
    return place, order


def return_tables():
    spread = np.zeros((PLACES * WIDE, LINES), np.float32)
    for i in range(PLACES):
        for w in range(WIDE):
            line = ROWS * w - EDGE + PLACE_ROWS[i]
            if 0 <= line < LINES:
                spread[i * WIDE + w, line] = 1.0
    rep = np.zeros((128, 2 * READOUT), np.float32)
    for i in range(2):
        for x in range(READOUT):
            rep[48 * i + x % COLS, i * READOUT + x] = 1.0
    pick = np.zeros((SLICES * 16, 2 * 6 * WIDE), np.float32)
    for i in range(2):
        for m in range(6):
            for w in range(WIDE):
                pick[(w // 16) * 16 + PLACE_ROWS[2 * m + i], (i * 6 + m) * WIDE + w] = 1.0
    return spread, rep, pick


def lane_iota(rows, lanes):
    return lax.broadcasted_iota(jnp.int32, (rows, lanes), 1)


def poly_sin(x):
    x2 = x * x
    return x * (1.0 + x2 * (-1.0 / 6 + x2 * (1.0 / 120 + x2 * (-1.0 / 5040 + x2 * (1.0 / 362880)))))


def poly_cos(x):
    x2 = x * x
    return 1.0 + x2 * (-0.5 + x2 * (1.0 / 24 + x2 * (-1.0 / 720 + x2 * (1.0 / 40320 - x2 * (1.0 / 3628800)))))


def tap_weights(frac):
    near = jnp.minimum(frac, 1.0 - frac) * (math.pi / 2)
    full = 2.0 * poly_sin(near) * poly_cos(near)
    phi = frac * (math.pi / 4)
    sin_a, cos_a = poly_sin(phi), poly_cos(phi)
    rest = (1.0 - frac) * (math.pi / 4)
    sin_b, cos_b = poly_sin(rest), poly_cos(rest)
    quarter = {-3: -sin_b, -2: -cos_a, -1: -cos_b, 0: -sin_a, 1: sin_b, 2: cos_a, 3: cos_b, 4: sin_a}
    weights = []
    for k in range(TAPS):
        n = k - 3
        t = n - frac
        sign = 1.0 if n % 2 else -1.0
        if n in (0, 1):
            small = jnp.abs(t) < 1e-5
            inverse = 1.0 / jnp.where(small, 1.0, t)
            product = (full * inverse) * (quarter[n] * inverse) * (sign * 4.0 / math.pi**2)
            weights.append(jnp.where(small, 1.0, product))
        else:
            inverse = 1.0 / t
            weights.append((full * inverse) * (quarter[n] * inverse) * (sign * 4.0 / math.pi**2))
    return weights


def wide_lines(values):
    return jnp.concatenate([values, jnp.zeros((values.shape[0], SPAN - LINES), F32)], axis=1)


def left(values, count):
    return pltpu.roll(values, (SPAN - count) % SPAN, 1) if count % SPAN else values


def split3(values):
    high = values.astype(BF16)
    rest = values - high.astype(F32)
    middle = rest.astype(BF16)
    low = (rest - middle.astype(F32)).astype(BF16)
    return high, middle, low


def dot(a, b):
    return jnp.dot(a, b, preferred_element_type=F32)


def dot_first(a, b):
    return lax.dot_general(a, b, (((0,), (0,)), ((), ())), preferred_element_type=F32)


def step_scalars(rr, ra, aa, ab):
    alpha = rr / (penalty * rr + ra)
    rho = ra / rr
    qq = jnp.maximum(aa - rho * ra, 0.0)
    qaq = ab - 2.0 * rho * aa + rho * rho * ra
    next_rr = alpha * alpha * qq
    beta = next_rr / rr
    direction_sq = next_rr + beta * beta * rr
    direction_a = alpha * alpha * qaq - 2.0 * beta * alpha * qq + beta * beta * ra
    image = jnp.maximum(penalty * direction_sq + direction_a, penalty * direction_sq)
    second = jnp.where(image > 0.0, next_rr / jnp.where(image > 0.0, image, 1.0), 0.0)
    return alpha + second * (alpha * rho + beta), -second * alpha


def whole_body(
    mask_any, kspace_any, frac_any, table_any, turned_any, place_any, order_any,
    spread_any, rep_any, pick_any, prior_any, maps_any, start_any,
    solution_ref, denoised_ref,
    mask_ref, kspace_ref, frac_ref, table_ref, turned_ref, place_ref, order_ref, spread_ref, rep_ref, pick_ref,
    prior_ref, maps_ref, start_ref,
    send_maps, got_ref, edge_ref, maps3_ref, weight_ref, data_ref, start_rows_ref,
    send_fields, got_fields, near_sum, far_sum, send_halo, got_halo, got_cross, send_dia, got_dia,
    load_sem, maps_sem, edge_send, edge_recv, field_sem, near_sem, far_sem, halo_send, halo_recv,
    cross_sem, near_cross, dia_sem,
):
    me = lax.axis_index("wide")
    nme = lax.axis_index("narrow")
    my_slice = me // 16
    both = 2 * COLS
    z_lo = me // 8
    got_halo[...] = jnp.zeros(got_halo.shape, BF16)
    got_cross[...] = jnp.zeros(got_cross.shape, F32)
    got_dia[...] = jnp.zeros(got_dia.shape, F32)
    barrier = pltpu.get_barrier_semaphore()

    def far_first(k):
        step = k // 8
        half = lax.rem(z_lo // 4 + 1 - step // 4 + 2, 2)
        return (4 * half + lax.rem(z_lo + 7 - step, 4)) * 8 + lax.rem(me + 7 - lax.rem(k, 8), 8)

    sources = (
        kspace_any, frac_any, table_any, turned_any, place_any, order_any, spread_any, rep_any, pick_any,
        prior_any, maps_any, start_any, mask_any,
    )
    targets = (
        kspace_ref, frac_ref, table_ref, turned_ref, place_ref, order_ref, spread_ref, rep_ref, pick_ref,
        prior_ref, maps_ref, start_ref, mask_ref,
    )
    loads = [pltpu.make_async_copy(a, b, load_sem.at[i]) for i, (a, b) in enumerate(zip(sources, targets))]
    for i in (9, 10, 11, 12, 1, 3, 0, 2, 4, 5, 6, 7, 8):
        loads[i].start()

    core, y_at = lax.rem(me, 2), lax.rem(me // 2, 4)
    x_at, z_hi = lax.rem(nme, 4), nme // 4
    z_at = z_hi * 8 + z_lo
    middle_pair = (nme == 3) | (nme == 4)
    across_to = NARROW - 1 - nme
    distance = jnp.where(nme == 3, SLICES - my_slice, my_slice + 1)
    crosses = middle_pair & (distance <= EDGE)

    def in_plane(a, b, c):
        wide_to = z_lo * 8 + lax.rem(y_at + b, 4) * 2 + lax.rem(core + c, 2)
        return {"wide": wide_to, "narrow": z_hi * 4 + lax.rem(x_at + a, 4)}

    def in_line(a):
        z_to = lax.rem(z_at + a, 16)
        return {"wide": lax.rem(z_to, 8) * 8 + lax.rem(me, 8), "narrow": (z_to // 8) * 4 + x_at}

    plane = [(a, b, c) for a in range(4) for b in range(4) for c in range(2) if (a, b, c) != (0, 0, 0)]
    plane.sort(key=lambda at: -(min(at[0], 4 - at[0]) + min(at[1], 4 - at[1])))
    line = sorted(range(1, 16), key=lambda a: -min(a, 16 - a))

    @pl.loop(1, 8)
    def _(k):
        other = {"wide": lax.rem(me + 8 * k, WIDE), "narrow": (1 - z_hi) * 4 + x_at}
        pl.semaphore_signal(barrier, inc=1, device_id=other, device_id_type=MESH)

    @pl.loop(1, NARROW)
    def _(k):
        pl.semaphore_signal(barrier, inc=1, device_id={"narrow": lax.rem(nme + k, NARROW)}, device_id_type=MESH)

    @pl.loop(0, WIDE - 1, unroll=9)
    def _(k):
        pl.semaphore_signal(barrier, inc=1, device_id={"wide": far_first(k)}, device_id_type=MESH)

    for a, b, c in plane:
        if a and (b or c):
            pl.semaphore_signal(barrier, inc=1, device_id=in_plane(a, b, c), device_id_type=MESH)

    loads[9].wait()
    loads[10].wait()
    lane8 = lane_iota(8, 128)
    stacked = [jnp.concatenate([prior_ref[t], prior_ref[3 + t]], axis=0) for t in range(3)]
    for q in range(16):
        packed = jnp.zeros((8, 128), F32)
        for t in range(3):
            turned = pltpu.roll(stacked[t], (24 * t - 24 * q) % READOUT, 1)[:, :128]
            packed = jnp.where((lane8 >= 24 * t) & (lane8 < 24 * t + 24), turned, packed)
        high = packed.astype(BF16).astype(F32)
        rest = packed - high
        middle = rest.astype(BF16).astype(F32)
        low = rest - middle
        packed = jnp.concatenate([high, middle, low], axis=1)
        for s in range(SLICES):
            d = 16 * s + q
            block = maps_ref[:, d * 384 : (d + 1) * 384].astype(F32)
            message = jnp.concatenate([block, packed[s : s + 1], packed[4 + s : 5 + s]], axis=0)
            send_maps[d] = message.astype(BF16)

    pl.semaphore_wait(barrier, WIDE + NARROW - 2 + 21 + 7)

    def to_wide(to, source, target, sems):
        pltpu.make_async_remote_copy(
            src_ref=source(to), dst_ref=target, send_sem=sems.at[0], recv_sem=sems.at[1],
            device_id={"wide": to}, device_id_type=MESH,
        ).start()

    def finish(source, target, sems, count):
        others = pl.ds(0, count)
        pltpu.make_async_copy(source.at[others], source.at[others], sems.at[0]).wait()
        pltpu.make_async_copy(target.at[others], target.at[others], sems.at[1]).wait()

    @pl.loop(1, WIDE, unroll=9)
    def _(k):
        to_wide(lax.rem(me + k, WIDE), lambda to: send_maps.at[to], got_ref.at[me], maps_sem)

    got_ref[me] = send_maps[me]

    edges = [
        pltpu.make_async_remote_copy(
            src_ref=prior_ref.at[pl.ds(first, EDGE)], dst_ref=edge_ref.at[side],
            send_sem=edge_send.at[side], recv_sem=edge_recv.at[side],
            device_id={"wide": lax.rem(me + step, WIDE)}, device_id_type=MESH,
        )
        for side, first, step in ((0, ROWS - EDGE, 1), (1, 0, WIDE - 1))
    ]
    for edge in edges:
        edge.start()

    loads[11].wait()
    loads[12].wait()
    starts = []
    diagonal = lax.broadcasted_iota(jnp.int32, (COLS, COLS), 0) == lax.broadcasted_iota(jnp.int32, (COLS, COLS), 1)
    for p in range(2):
        row = jnp.broadcast_to(start_ref[p : p + 1, :].astype(F32), (COLS, COLS))
        starts.append(jnp.sum(jnp.where(diagonal, row, 0.0), axis=1, keepdims=True))
    ahead = jnp.concatenate(starts, axis=0).astype(jnp.int32) + 12
    start_rows_ref[...] = jnp.broadcast_to(ahead, (both, SPAN))

    loads[1].wait()
    frac = jnp.concatenate([frac_ref[0], frac_ref[1]], axis=0)
    for k, weight in enumerate(tap_weights(frac)):
        weight_ref[k] = weight

    shot = lax.rem(lane_iota(1, LINES), SHOTS)
    masks = []
    for p in range(2):
        row = jnp.zeros((1, LINES), F32)
        for h in range(SHOTS):
            row = jnp.where(shot == h, mask_ref[p, my_slice, h].astype(F32), row)
        masks.append(row)
    loads[3].wait()
    turned = turned_ref[...].astype(F32)
    forward = [(turned * masks[p]).astype(BF16) for p in range(2)]
    loads[0].wait()
    for p in range(2):
        data_ref[p] = lax.dot_general(
            kspace_ref[p], forward[p], (((0,), (1,)), ((), ())), preferred_element_type=F32
        )
    for i in (2, 4, 5, 6, 7, 8):
        loads[i].wait()

    for edge in edges:
        edge.wait()
    below = jnp.where(me > 0, 1.0, 0.0).astype(F32)
    above = jnp.where(me < WIDE - 1, 1.0, 0.0).astype(F32)
    cells = []
    for s in range(SLICES):
        rows = [edge_ref[0, i, s : s + 1, :] * below for i in range(EDGE)]
        rows += [prior_ref[i, s : s + 1, :] for i in range(ROWS)]
        rows += [edge_ref[1, i, s : s + 1, :] * above for i in range(EDGE)]
        rows += [jnp.zeros((16 - PLACES, READOUT), F32)]
        cells.append(jnp.concatenate(rows, axis=0))

    def diamond(near, middle, far):
        return jnp.concatenate([near[1:11], middle[2:10], far[3:9]], axis=0)

    send_dia[...] = jnp.where(nme == 3, diamond(cells[3], cells[2], cells[1]), diamond(cells[0], cells[1], cells[2]))
    dia = pltpu.make_async_remote_copy(
        src_ref=send_dia, dst_ref=got_dia, send_sem=dia_sem.at[0], recv_sem=dia_sem.at[1],
        device_id={"narrow": across_to}, device_id_type=MESH,
    )

    @pl.when(middle_pair)
    def _():
        dia.start()

    finish(send_maps, got_ref, maps_sem, WIDE - 1)
    got = got_ref[...].reshape(WIDE * 8, LINES)
    laid = dot_first(got, place_ref[...])
    maps3_ref[...] = laid[:, :LINES].reshape(COLS, COILS, LINES)
    pieces = []
    for m in range(PIECES):
        parts = [laid[m * 128 + 24 * t : m * 128 + 24 * t + 24, LINES:] for t in range(3)]
        pieces.append(jnp.concatenate(parts, axis=1))
    ordered = dot(jnp.concatenate(pieces, axis=0).astype(BF16), order_ref[...])
    prior = ordered[:COLS] + ordered[COLS : 2 * COLS] + ordered[2 * COLS :]

    def bit_set(bit):
        return ((start_rows_ref[...] >> bit) & 1) == 1

    def band_apply(field):
        value = wide_lines(jnp.concatenate([field, field], axis=0))
        value = left(value, -15)
        for bit in range(BAND_BITS):
            value = jnp.where(bit_set(bit), left(value, 1 << bit), value)
        total = jnp.zeros((both, LINES), F32)
        for k in range(TAPS):
            total = total + weight_ref[k] * left(value, k)[:, :LINES]
        return total

    def band_adjoint(values):
        total = jnp.zeros((both, SPAN), F32)
        for k in range(TAPS):
            total = total + left(wide_lines(weight_ref[k] * values), -k)
        for bit in range(BAND_BITS):
            total = jnp.where(bit_set(bit), left(total, -(1 << bit)), total)
        total = left(total, 15)
        return (total[:COLS] + total[COLS:])[:, :LINES]

    def spectra(moved, p):
        image = maps3_ref[...] * moved[p * COLS : (p + 1) * COLS][:, None, :]
        return dot(image.reshape(COLS * COILS, LINES).astype(BF16), forward[p])

    def combine(back):
        return jnp.sum(back.reshape(COLS, COILS, LINES) * maps3_ref[...], axis=1)

    def through(field):
        moved = band_apply(field)
        return [dot(spectra(moved, p).astype(BF16), table_ref[...]) for p in range(2)]

    back = through(prior)
    residue = band_adjoint(jnp.concatenate([combine(data_ref[p] - back[p]) for p in range(2)], axis=0))
    back = through(residue)
    first = band_adjoint(jnp.concatenate([combine(back[p]) for p in range(2)], axis=0))

    moved = band_apply(first)
    squares = jnp.zeros((1, LINES), F32)
    for p in range(2):
        here = spectra(moved, p)
        squares = squares + jnp.sum(here * here.astype(BF16).astype(F32), axis=0, keepdims=True)

    def total(values):
        return jnp.sum(jnp.sum(values, axis=0, keepdims=True), axis=1, keepdims=True)

    lane1 = lane_iota(1, 128)
    sums = jnp.zeros((1, 128), F32)
    for i, part in enumerate((residue * residue, residue * first, first * first, squares)):
        sums = jnp.where(lane1 == i, total(part), sums)
    in_plane_at = x_at * 8 + lax.rem(me, 8)
    near_sum[in_plane_at] = sums

    def to_device(ref, slot, sems, device):
        pltpu.make_async_remote_copy(
            src_ref=ref.at[slot], dst_ref=ref.at[slot], send_sem=sems.at[0], recv_sem=sems.at[1],
            device_id=device, device_id_type=MESH,
        ).start()

    for at in plane:
        to_device(near_sum, in_plane_at, near_sem, in_plane(*at))

    fields = jnp.concatenate([residue, first, jnp.zeros((128 - 2 * COLS, LINES), F32)], axis=0)
    high = fields.astype(BF16)
    low = (fields - high.astype(F32)).astype(BF16)
    across = (((1,), (1,)), ((), ()))
    placed = lax.dot_general(spread_ref[...], high, across, preferred_element_type=F32)
    placed = placed + lax.dot_general(spread_ref[...], low, across, preferred_element_type=F32)
    lane = lane_iota(WIDE, 128)
    for row in range(DENSE):
        packed = jnp.zeros((WIDE, 128), F32)
        for i in range(PLACES):
            begin = 48 * i - 128 * row
            if begin < 128 and begin + 48 > 0:
                turned = placed[i * WIDE : (i + 1) * WIDE]
                if begin % 128:
                    turned = pltpu.roll(turned, begin % 128, 1)
                packed = jnp.where((lane >= begin) & (lane < begin + 48), turned, packed)
        send_fields[:, row, :] = packed

    @pl.loop(0, WIDE // 2, unroll=8)
    def _(k):
        to_wide(far_first(k), lambda to: send_fields.at[to], got_fields.at[me], field_sem)

    finish(near_sum, near_sum, near_sem, PLANE - 1)
    far_sum[z_at] = jnp.sum(near_sum[...].reshape(PLANE, 128), axis=0, keepdims=True)
    for at in line:
        to_device(far_sum, z_at, far_sem, in_line(at))

    @pl.loop(WIDE // 2, WIDE - 1)
    def _(k):
        to_wide(far_first(k), lambda to: send_fields.at[to], got_fields.at[me], field_sem)

    def cross(rows, sems):
        @pl.loop(0, WIDE, unroll=8)
        def _(k):
            step = k // 8
            ahead_by = jnp.where(lax.rem(step, 2) == 1, (step + 1) // 2, 8 - step // 2)
            to = lax.rem(z_lo + ahead_by, 8) * 8 + lax.rem(me + 4 + k, 8)
            pltpu.make_async_remote_copy(
                src_ref=send_fields.at[to, pl.ds(0, rows)], dst_ref=got_cross.at[me, pl.ds(0, rows)],
                send_sem=sems.at[0], recv_sem=sems.at[1],
                device_id={"wide": to, "narrow": across_to}, device_id_type=MESH,
            ).start()

    @pl.when(crosses & (distance == 1))
    def _():
        cross(4, near_cross)

    @pl.when(crosses & (distance > 1))
    def _():
        cross(3, cross_sem)

    got_fields[me] = send_fields[me]

    finish(far_sum, far_sum, far_sem, LINE - 1)
    sums = jnp.sum(far_sum[...].reshape(LINE, 128), axis=0, keepdims=True)
    picked = [jnp.sum(jnp.where(lane1 == i, sums, 0.0), axis=1, keepdims=True) for i in range(4)]
    c0, c1 = step_scalars(*picked)
    solution_ref[...] = prior + c0 * residue + c1 * first

    finish(send_fields, got_fields, field_sem, WIDE - 1)
    def unpack(source):
        lines = [source[:, row, :] for row in range(DENSE)]
        pairs = []
        for m in range(6):
            begin = 96 * m
            row, off = begin // 128, begin % 128
            pair = pltpu.roll(lines[row], 128 - off, 1) if off else lines[row]
            if off + 96 > 128:
                pair = jnp.where(lane < 128 - off, pair, pltpu.roll(lines[row + 1], 128 - off, 1))
            pairs.append(pair)
        pairs = jnp.concatenate(pairs, axis=0)
        joined = c0 * pairs + c1 * pltpu.roll(pairs, 128 - COLS, 1)
        high = joined.astype(BF16)
        low = (joined - high.astype(F32)).astype(BF16)
        block_of = lax.broadcasted_iota(jnp.int32, (16, 2 * READOUT), 0)
        readout_of = lax.rem(lane_iota(16, 2 * READOUT), READOUT)
        inside = (readout_of >= COLS * block_of) & (readout_of < COLS * block_of + COLS)
        change = jnp.zeros((SLICES * 16, READOUT), F32)
        for part in (high, low):
            wide = dot(part, rep_ref[...]).reshape(6 * SLICES, 16, 2 * READOUT)
            wide = jnp.where(inside[None], wide, 0.0).reshape(6 * WIDE, 2 * READOUT).astype(BF16)
            wide = jnp.concatenate([wide[:, :READOUT], wide[:, READOUT:]], axis=0)
            change = change + dot(pick_ref[...], wide)
        return [change[16 * s : 16 * s + 16] for s in range(SLICES)]

    change = unpack(got_fields)
    cells = [cells[s] + change[s] for s in range(SLICES)]

    send_halo[0] = diamond(cells[3], cells[2], cells[1]).astype(BF16)
    send_halo[1] = diamond(cells[0], cells[1], cells[2]).astype(BF16)
    up, down = (
        pltpu.make_async_remote_copy(
            src_ref=send_halo.at[side], dst_ref=got_halo.at[side],
            send_sem=halo_send.at[side], recv_sem=halo_recv.at[side],
            device_id={"narrow": lax.rem(nme + step, NARROW)}, device_id_type=MESH,
        )
        for side, step in ((0, 1), (1, NARROW - 1))
    )

    @pl.when(x_at < 3)
    def _():
        up.start()

    @pl.when(x_at > 0)
    def _():
        down.start()

    def wait_cross(ref, count, rows, sem):
        part = ref.at[pl.ds(0, count), pl.ds(0, rows)]
        pltpu.make_async_copy(part, part, sem).wait()

    @pl.when(crosses & (distance == 1))
    def _():
        wait_cross(send_fields, WIDE, 4, near_cross.at[0])

    @pl.when(crosses & (distance > 1))
    def _():
        wait_cross(send_fields, WIDE, 3, cross_sem.at[0])

    @pl.when(middle_pair)
    def _():
        dia.wait()
        wait_cross(got_cross, 16, 4, near_cross.at[1])
        wait_cross(got_cross, 32, 3, cross_sem.at[1])

    crossed = unpack(got_cross)
    crossed = jnp.where(
        nme == 3, diamond(crossed[0], crossed[1], crossed[2]), diamond(crossed[3], crossed[2], crossed[1])
    )
    crossed = crossed + got_dia[...]

    @pl.when(x_at < 3)
    def _():
        up.wait_send()
        down.wait_recv()

    @pl.when(x_at > 0)
    def _():
        down.wait_send()
        up.wait_recv()

    def opened(rows):
        zero = jnp.zeros((8, READOUT), F32)
        near = jnp.concatenate([zero[:1], rows[:10], zero[:5]], axis=0)
        middle = jnp.concatenate([zero[:2], rows[10:18], zero[:6]], axis=0)
        far = jnp.concatenate([zero[:3], rows[18:24], zero[:7]], axis=0)
        return near, middle, far

    has_low = jnp.where(nme > 0, 1.0, 0.0).astype(F32)
    has_high = jnp.where(nme < NARROW - 1, 1.0, 0.0).astype(F32)
    near_low, mid_low, far_low = opened(jnp.where(nme == 4, crossed, got_halo[0].astype(F32)))
    near_high, mid_high, far_high = opened(jnp.where(nme == 3, crossed, got_halo[1].astype(F32)))
    volume = [far_low, mid_low, near_low] + cells + [near_high, mid_high, far_high]
    keeps = [has_low] * 3 + [None] * SLICES + [has_high] * 3
    margin = jnp.zeros((16, 128), F32)
    volume = [jnp.concatenate([one, margin], axis=1) for one in volume]
    line_of = lax.broadcasted_iota(jnp.int32, (16, READOUT + 128), 0) + (ROWS * me - EDGE)
    in_grid = (line_of >= 0) & (line_of < LINES) & (lane_iota(16, READOUT + 128) < READOUT)
    in_grid = in_grid.astype(F32)

    def flux(jump):
        return jump / (1.0 + jump * jump)

    for step in range(DIFF_STEPS):
        last = len(volume) - 1
        across_slices = [flux(volume[i + 1] - volume[i]) for i in range(last)]
        after = []
        for i in range(1, last):
            one = volume[i]
            down = flux(pltpu.roll(one, 15, 0) - one)
            along = flux(pltpu.roll(one, SPAN - 1, 1) - one)
            moved = axis_weights[0] * (down - pltpu.roll(down, 1, 0))
            moved = moved + axis_weights[1] * (across_slices[i] - across_slices[i - 1])
            moved = moved + axis_weights[2] * (along - pltpu.roll(along, 1, 1))
            grid = in_grid if keeps[i] is None else in_grid * keeps[i]
            after.append((one + time_step * moved) * grid)
        volume = after
        keeps = keeps[1:-1]
    for s in range(SLICES):
        for i in range(ROWS):
            denoised_ref[i, s : s + 1, :] = volume[s][EDGE + i : EDGE + i + 1, :READOUT]


def whole(prior, coil_maps, kspace, band_start, frac, mask):
    vmem = pl.BlockSpec(memory_space=pltpu.VMEM)
    far = pl.BlockSpec(memory_space=pltpu.HBM)
    table = cosine_table()
    constants = (table, table.T) + place_tables() + return_tables()
    constants = [jnp.asarray(one, BF16) for one in constants]
    moved = [kspace, frac] + constants + [prior, coil_maps, band_start]
    return pl.pallas_call(
        whole_body,
        out_shape=(
            jax.ShapeDtypeStruct((COLS, LINES), F32),
            jax.ShapeDtypeStruct((ROWS, SLICES, READOUT), F32),
        ),
        in_specs=[far] * (len(moved) + 1),
        out_specs=(vmem, vmem),
        scratch_shapes=[pltpu.SMEM(mask.shape, mask.dtype)]
        + [pltpu.VMEM(one.shape, one.dtype) for one in moved]
        + [
            pltpu.VMEM((WIDE, 8, LINES), BF16),
            pltpu.VMEM((WIDE, 8, LINES), BF16),
            pltpu.VMEM((2, EDGE, SLICES, READOUT), F32),
            pltpu.VMEM((COLS, COILS, LINES), F32),
            pltpu.VMEM((TAPS, 2 * COLS, LINES), F32),
            pltpu.VMEM((2, COLS * COILS, LINES), F32),
            pltpu.VMEM((2 * COLS, SPAN), jnp.int32),
            pltpu.VMEM((WIDE, DENSE, 128), F32),
            pltpu.VMEM((WIDE, DENSE, 128), F32),
            pltpu.VMEM((PLANE, 1, 128), F32),
            pltpu.VMEM((LINE, 1, 128), F32),
            pltpu.VMEM((2, HALO, READOUT), BF16),
            pltpu.VMEM((2, HALO, READOUT), BF16),
            pltpu.VMEM((WIDE, DENSE, 128), F32),
            pltpu.VMEM((HALO, READOUT), F32),
            pltpu.VMEM((HALO, READOUT), F32),
            pltpu.SemaphoreType.DMA((len(moved) + 1,)),
            pltpu.SemaphoreType.DMA((2,)),
            pltpu.SemaphoreType.DMA((2,)),
            pltpu.SemaphoreType.DMA((2,)),
            pltpu.SemaphoreType.DMA((2,)),
            pltpu.SemaphoreType.DMA((2,)),
            pltpu.SemaphoreType.DMA((2,)),
            pltpu.SemaphoreType.DMA((2,)),
            pltpu.SemaphoreType.DMA((2,)),
            pltpu.SemaphoreType.DMA((2,)),
            pltpu.SemaphoreType.DMA((2,)),
            pltpu.SemaphoreType.DMA((2,)),
        ],
        compiler_params=pltpu.CompilerParams(collective_id=0, has_side_effects=True, vmem_limit_bytes=63 << 20),
        name="whole",
    )(mask, *moved)


def per_device(prior, coil_maps, kspace, band_start, band_frac, shot_mask):
    solved, denoised = whole(
        prior, coil_maps, kspace, band_start, jnp.transpose(band_frac, (0, 2, 1)), jnp.transpose(shot_mask, (0, 2, 1))
    )
    return jnp.transpose(solved), denoised


def solution(mesh):
    in_specs = (
        P("wide", "narrow", None),
        P("wide", "narrow"),
        P(None, None, ("narrow", "wide")),
        P(None, ("narrow", "wide")),
        P(None, None, ("narrow", "wide")),
        P(None, None, "narrow"),
    )
    out_specs = (P(None, ("narrow", "wide")), P("wide", "narrow", None))
    return jax.shard_map(per_device, mesh=mesh, in_specs=in_specs, out_specs=out_specs, check_vma=False)
```

```python
import functools
import math

import jax
import jax.numpy as jnp
import numpy as np
from jax import lax
from jax.experimental import pallas as pl
from jax.experimental.pallas import tpu as pltpu
from jax.sharding import PartitionSpec as P

SHOTS = 6
TAPS = 8
DIFF_STEPS = 3
COILS = 16
WIDE = 64
NARROW = 8
PLANE = 32
LINE = 16
LINES = 384
COLS = 24
ROWS = 6
SLICES = 4
READOUT = 384
SPAN = 512
PIECES = 3
EDGE = DIFF_STEPS
PLACES = ROWS + 2 * EDGE
PLACE_ROWS = (3, 4, 5, 6, 7, 8, 2, 9, 1, 10, 0, 11)
DENSE = 5
HALO = 24
BAND_BITS = 5

penalty = 0.5
time_step = 0.18
axis_weights = (1.0, 0.5, 1.0)

F32 = jnp.float32
BF16 = jnp.bfloat16
MESH = pl.DeviceIdType.MESH


def cosine_table():
    freq = np.arange(LINES, dtype=np.float32)[:, None]
    cell = np.arange(LINES, dtype=np.float32)[None, :]
    angle = np.float32(math.pi) * (cell + np.float32(0.5)) * freq / np.float32(LINES)
    entries = np.cos(angle).astype(np.float32) * np.float32(math.sqrt(2.0 / LINES))
    entries = entries * np.where(freq == 0.0, np.float32(math.sqrt(0.5)), np.float32(1.0))
    return entries.astype(np.float32)


def place_tables():
    place = np.zeros((WIDE * 8, LINES + 128), np.float32)
    for w in range(WIDE):
        for i in range(ROWS):
            place[8 * w + i, ROWS * w + i] = 1.0
        for g in range(2):
            place[8 * w + 6 + g, LINES + g * 64 + w] = 1.0
    order = np.zeros((3 * 128, LINES), np.float32)
    for t in range(3):
        for g in range(2):
            for w in range(WIDE):
                order[t * 128 + g * 64 + w, ROWS * w + 3 * g + t] = 1.0
    return place, order


def return_tables():
    spread = np.zeros((PLACES * WIDE, LINES), np.float32)
    for i in range(PLACES):
        for w in range(WIDE):
            line = ROWS * w - EDGE + PLACE_ROWS[i]
            if 0 <= line < LINES:
                spread[i * WIDE + w, line] = 1.0
    rep = np.zeros((128, 2 * READOUT), np.float32)
    for i in range(2):
        for x in range(READOUT):
            rep[48 * i + x % COLS, i * READOUT + x] = 1.0
    pick = np.zeros((SLICES * 16, 2 * 6 * WIDE), np.float32)
    for i in range(2):
        for m in range(6):
            for w in range(WIDE):
                pick[(w // 16) * 16 + PLACE_ROWS[2 * m + i], (i * 6 + m) * WIDE + w] = 1.0
    return spread, rep, pick


def lane_iota(rows, lanes):
    return lax.broadcasted_iota(jnp.int32, (rows, lanes), 1)


def poly_sin(x):
    x2 = x * x
    return x * (1.0 + x2 * (-1.0 / 6 + x2 * (1.0 / 120 + x2 * (-1.0 / 5040 + x2 * (1.0 / 362880)))))


def poly_cos(x):
    x2 = x * x
    return 1.0 + x2 * (-0.5 + x2 * (1.0 / 24 + x2 * (-1.0 / 720 + x2 * (1.0 / 40320 - x2 * (1.0 / 3628800)))))


def tap_weights(frac):
    near = jnp.minimum(frac, 1.0 - frac) * (math.pi / 2)
    full = 2.0 * poly_sin(near) * poly_cos(near)
    phi = frac * (math.pi / 4)
    sin_a, cos_a = poly_sin(phi), poly_cos(phi)
    rest = (1.0 - frac) * (math.pi / 4)
    sin_b, cos_b = poly_sin(rest), poly_cos(rest)
    quarter = {-3: -sin_b, -2: -cos_a, -1: -cos_b, 0: -sin_a, 1: sin_b, 2: cos_a, 3: cos_b, 4: sin_a}
    weights = []
    for k in range(TAPS):
        n = k - 3
        t = n - frac
        sign = 1.0 if n % 2 else -1.0
        if n in (0, 1):
            small = jnp.abs(t) < 1e-5
            inverse = 1.0 / jnp.where(small, 1.0, t)
            product = (full * inverse) * (quarter[n] * inverse) * (sign * 4.0 / math.pi**2)
            weights.append(jnp.where(small, 1.0, product))
        else:
            inverse = 1.0 / t
            weights.append((full * inverse) * (quarter[n] * inverse) * (sign * 4.0 / math.pi**2))
    return weights


def wide_lines(values):
    return jnp.concatenate([values, jnp.zeros((values.shape[0], SPAN - LINES), F32)], axis=1)


def left(values, count):
    return pltpu.roll(values, (SPAN - count) % SPAN, 1) if count % SPAN else values


def split3(values):
    high = values.astype(BF16)
    rest = values - high.astype(F32)
    middle = rest.astype(BF16)
    low = (rest - middle.astype(F32)).astype(BF16)
    return high, middle, low


def dot(a, b):
    return jnp.dot(a, b, preferred_element_type=F32)


def dot_first(a, b):
    return lax.dot_general(a, b, (((0,), (0,)), ((), ())), preferred_element_type=F32)


def step_scalars(rr, ra, aa, ab):
    alpha = rr / (penalty * rr + ra)
    rho = ra / rr
    qq = jnp.maximum(aa - rho * ra, 0.0)
    qaq = ab - 2.0 * rho * aa + rho * rho * ra
    next_rr = alpha * alpha * qq
    beta = next_rr / rr
    direction_sq = next_rr + beta * beta * rr
    direction_a = alpha * alpha * qaq - 2.0 * beta * alpha * qq + beta * beta * ra
    image = jnp.maximum(penalty * direction_sq + direction_a, penalty * direction_sq)
    second = jnp.where(image > 0.0, next_rr / jnp.where(image > 0.0, image, 1.0), 0.0)
    return alpha + second * (alpha * rho + beta), -second * alpha


def whole_body(
    mask_any, kspace_any, frac_any, table_any, turned_any, place_any, order_any,
    spread_any, rep_any, pick_any, prior_any, maps_any, start_any,
    solution_ref, denoised_ref,
    mask_ref, kspace_ref, frac_ref, table_ref, turned_ref, place_ref, order_ref, spread_ref, rep_ref, pick_ref,
    prior_ref, maps_ref, start_ref,
    send_maps, got_ref, edge_ref, maps3_ref, weight_ref, data_ref, start_rows_ref,
    send_fields, got_fields, near_sum, far_sum, send_halo, got_halo, got_cross, send_dia, got_dia,
    load_sem, maps_sem, edge_send, edge_recv, field_sem, near_sem, far_sem, halo_send, halo_recv,
    cross_sem, near_cross, dia_sem,
):
    me = lax.axis_index("wide")
    nme = lax.axis_index("narrow")
    my_slice = me // 16
    both = 2 * COLS
    z_lo = me // 8
    got_halo[...] = jnp.zeros(got_halo.shape, BF16)
    got_cross[...] = jnp.zeros(got_cross.shape, F32)
    got_dia[...] = jnp.zeros(got_dia.shape, F32)
    barrier = pltpu.get_barrier_semaphore()

    def far_first(k):
        step = k // 8
        half = lax.rem(z_lo // 4 + 1 - step // 4 + 2, 2)
        return (4 * half + lax.rem(z_lo + 7 - step, 4)) * 8 + lax.rem(me + 7 - lax.rem(k, 8), 8)

    sources = (
        kspace_any, frac_any, table_any, turned_any, place_any, order_any, spread_any, rep_any, pick_any,
        prior_any, maps_any, start_any, mask_any,
    )
    targets = (
        kspace_ref, frac_ref, table_ref, turned_ref, place_ref, order_ref, spread_ref, rep_ref, pick_ref,
        prior_ref, maps_ref, start_ref, mask_ref,
    )
    loads = [pltpu.make_async_copy(a, b, load_sem.at[i]) for i, (a, b) in enumerate(zip(sources, targets))]
    for i in (9, 10):
        loads[i].start()

    core, y_at = lax.rem(me, 2), lax.rem(me // 2, 4)
    x_at, z_hi = lax.rem(nme, 4), nme // 4
    z_at = z_hi * 8 + z_lo
    middle_pair = (nme == 3) | (nme == 4)
    across_to = NARROW - 1 - nme
    distance = jnp.where(nme == 3, SLICES - my_slice, my_slice + 1)
    crosses = middle_pair & (distance <= EDGE)

    def in_plane(a, b, c):
        wide_to = z_lo * 8 + lax.rem(y_at + b, 4) * 2 + lax.rem(core + c, 2)
        return {"wide": wide_to, "narrow": z_hi * 4 + lax.rem(x_at + a, 4)}

    def in_line(a):
        z_to = lax.rem(z_at + a, 16)
        return {"wide": lax.rem(z_to, 8) * 8 + lax.rem(me, 8), "narrow": (z_to // 8) * 4 + x_at}

    plane = [(a, b, c) for a in range(4) for b in range(4) for c in range(2) if (a, b, c) != (0, 0, 0)]
    plane.sort(key=lambda at: -(min(at[0], 4 - at[0]) + min(at[1], 4 - at[1])))
    line = sorted(range(1, 16), key=lambda a: -min(a, 16 - a))

    @pl.loop(1, 8)
    def _(k):
        other = {"wide": lax.rem(me + 8 * k, WIDE), "narrow": (1 - z_hi) * 4 + x_at}
        pl.semaphore_signal(barrier, inc=1, device_id=other, device_id_type=MESH)

    @pl.loop(1, NARROW)
    def _(k):
        pl.semaphore_signal(barrier, inc=1, device_id={"narrow": lax.rem(nme + k, NARROW)}, device_id_type=MESH)

    @pl.loop(0, WIDE - 1, unroll=9)
    def _(k):
        pl.semaphore_signal(barrier, inc=1, device_id={"wide": far_first(k)}, device_id_type=MESH)

    for a, b, c in plane:
        if a and (b or c):
            pl.semaphore_signal(barrier, inc=1, device_id=in_plane(a, b, c), device_id_type=MESH)

    for i in (11, 12, 1, 3, 0, 2, 4, 5, 6, 7, 8):
        loads[i].start()

    loads[9].wait()
    loads[10].wait()
    lane8 = lane_iota(8, 128)
    stacked = [jnp.concatenate([prior_ref[t], prior_ref[3 + t]], axis=0) for t in range(3)]
    for q in range(16):
        packed = jnp.zeros((8, 128), F32)
        for t in range(3):
            turned = pltpu.roll(stacked[t], (24 * t - 24 * q) % READOUT, 1)[:, :128]
            packed = jnp.where((lane8 >= 24 * t) & (lane8 < 24 * t + 24), turned, packed)
        high = packed.astype(BF16).astype(F32)
        rest = packed - high
        middle = rest.astype(BF16).astype(F32)
        low = rest - middle
        packed = jnp.concatenate([high, middle, low], axis=1)
        for s in range(SLICES):
            d = 16 * s + q
            block = maps_ref[:, d * 384 : (d + 1) * 384].astype(F32)
            message = jnp.concatenate([block, packed[s : s + 1], packed[4 + s : 5 + s]], axis=0)
            send_maps[d] = message.astype(BF16)

    pl.semaphore_wait(barrier, WIDE + NARROW - 2 + 21 + 7)

    def to_wide(to, source, target, sems):
        pltpu.make_async_remote_copy(
            src_ref=source(to), dst_ref=target, send_sem=sems.at[0], recv_sem=sems.at[1],
            device_id={"wide": to}, device_id_type=MESH,
        ).start()

    def finish(source, target, sems, count):
        others = pl.ds(0, count)
        pltpu.make_async_copy(source.at[others], source.at[others], sems.at[0]).wait()
        pltpu.make_async_copy(target.at[others], target.at[others], sems.at[1]).wait()

    @pl.loop(1, WIDE, unroll=9)
    def _(k):
        to_wide(lax.rem(me + k, WIDE), lambda to: send_maps.at[to], got_ref.at[me], maps_sem)

    got_ref[me] = send_maps[me]

    edges = [
        pltpu.make_async_remote_copy(
            src_ref=prior_ref.at[pl.ds(first, EDGE)], dst_ref=edge_ref.at[side],
            send_sem=edge_send.at[side], recv_sem=edge_recv.at[side],
            device_id={"wide": lax.rem(me + step, WIDE)}, device_id_type=MESH,
        )
        for side, first, step in ((0, ROWS - EDGE, 1), (1, 0, WIDE - 1))
    ]
    for edge in edges:
        edge.start()

    loads[11].wait()
    loads[12].wait()
    starts = []
    diagonal = lax.broadcasted_iota(jnp.int32, (COLS, COLS), 0) == lax.broadcasted_iota(jnp.int32, (COLS, COLS), 1)
    for p in range(2):
        row = jnp.broadcast_to(start_ref[p : p + 1, :].astype(F32), (COLS, COLS))
        starts.append(jnp.sum(jnp.where(diagonal, row, 0.0), axis=1, keepdims=True))
    ahead = jnp.concatenate(starts, axis=0).astype(jnp.int32) + 12
    start_rows_ref[...] = jnp.broadcast_to(ahead, (both, SPAN))

    loads[1].wait()
    frac = jnp.concatenate([frac_ref[0], frac_ref[1]], axis=0)
    for k, weight in enumerate(tap_weights(frac)):
        weight_ref[k] = weight

    shot = lax.rem(lane_iota(1, LINES), SHOTS)
    masks = []
    for p in range(2):
        row = jnp.zeros((1, LINES), F32)
        for h in range(SHOTS):
            row = jnp.where(shot == h, mask_ref[p, my_slice, h].astype(F32), row)
        masks.append(row)
    loads[3].wait()
    turned = turned_ref[...].astype(F32)
    forward = [(turned * masks[p]).astype(BF16) for p in range(2)]
    loads[0].wait()
    for p in range(2):
        data_ref[p] = lax.dot_general(
            kspace_ref[p], forward[p], (((0,), (1,)), ((), ())), preferred_element_type=F32
        )
    for i in (2, 4, 5, 6, 7, 8):
        loads[i].wait()

    for edge in edges:
        edge.wait()
    below = jnp.where(me > 0, 1.0, 0.0).astype(F32)
    above = jnp.where(me < WIDE - 1, 1.0, 0.0).astype(F32)
    cells = []
    for s in range(SLICES):
        rows = [edge_ref[0, i, s : s + 1, :] * below for i in range(EDGE)]
        rows += [prior_ref[i, s : s + 1, :] for i in range(ROWS)]
        rows += [edge_ref[1, i, s : s + 1, :] * above for i in range(EDGE)]
        rows += [jnp.zeros((16 - PLACES, READOUT), F32)]
        cells.append(jnp.concatenate(rows, axis=0))

    def diamond(near, middle, far):
        return jnp.concatenate([near[1:11], middle[2:10], far[3:9]], axis=0)

    send_dia[...] = jnp.where(nme == 3, diamond(cells[3], cells[2], cells[1]), diamond(cells[0], cells[1], cells[2]))
    dia = pltpu.make_async_remote_copy(
        src_ref=send_dia, dst_ref=got_dia, send_sem=dia_sem.at[0], recv_sem=dia_sem.at[1],
        device_id={"narrow": across_to}, device_id_type=MESH,
    )

    @pl.when(middle_pair)
    def _():
        dia.start()

    finish(send_maps, got_ref, maps_sem, WIDE - 1)
    got = got_ref[...].reshape(WIDE * 8, LINES)
    laid = dot_first(got, place_ref[...])
    maps3_ref[...] = laid[:, :LINES].reshape(COLS, COILS, LINES)
    pieces = []
    for m in range(PIECES):
        parts = [laid[m * 128 + 24 * t : m * 128 + 24 * t + 24, LINES:] for t in range(3)]
        pieces.append(jnp.concatenate(parts, axis=1))
    ordered = dot(jnp.concatenate(pieces, axis=0).astype(BF16), order_ref[...])
    prior = ordered[:COLS] + ordered[COLS : 2 * COLS] + ordered[2 * COLS :]

    def bit_set(bit):
        return ((start_rows_ref[...] >> bit) & 1) == 1

    def band_apply(field):
        value = wide_lines(jnp.concatenate([field, field], axis=0))
        value = left(value, -15)
        for bit in range(BAND_BITS):
            value = jnp.where(bit_set(bit), left(value, 1 << bit), value)
        total = jnp.zeros((both, LINES), F32)
        for k in range(TAPS):
            total = total + weight_ref[k] * left(value, k)[:, :LINES]
        return total

    def band_adjoint(values):
        total = jnp.zeros((both, SPAN), F32)
        for k in range(TAPS):
            total = total + left(wide_lines(weight_ref[k] * values), -k)
        for bit in range(BAND_BITS):
            total = jnp.where(bit_set(bit), left(total, -(1 << bit)), total)
        total = left(total, 15)
        return (total[:COLS] + total[COLS:])[:, :LINES]

    def spectra(moved, p):
        image = maps3_ref[...] * moved[p * COLS : (p + 1) * COLS][:, None, :]
        return dot(image.reshape(COLS * COILS, LINES).astype(BF16), forward[p])

    def combine(back):
        return jnp.sum(back.reshape(COLS, COILS, LINES) * maps3_ref[...], axis=1)

    def through(field):
        moved = band_apply(field)
        return [dot(spectra(moved, p).astype(BF16), table_ref[...]) for p in range(2)]

    back = through(prior)
    residue = band_adjoint(jnp.concatenate([combine(data_ref[p] - back[p]) for p in range(2)], axis=0))
    back = through(residue)
    first = band_adjoint(jnp.concatenate([combine(back[p]) for p in range(2)], axis=0))

    moved = band_apply(first)
    squares = jnp.zeros((1, LINES), F32)
    for p in range(2):
        here = spectra(moved, p)
        squares = squares + jnp.sum(here * here.astype(BF16).astype(F32), axis=0, keepdims=True)

    def total(values):
        return jnp.sum(jnp.sum(values, axis=0, keepdims=True), axis=1, keepdims=True)

    lane1 = lane_iota(1, 128)
    sums = jnp.zeros((1, 128), F32)
    for i, part in enumerate((residue * residue, residue * first, first * first, squares)):
        sums = jnp.where(lane1 == i, total(part), sums)
    in_plane_at = x_at * 8 + lax.rem(me, 8)
    near_sum[in_plane_at] = sums

    def to_device(ref, slot, sems, device):
        pltpu.make_async_remote_copy(
            src_ref=ref.at[slot], dst_ref=ref.at[slot], send_sem=sems.at[0], recv_sem=sems.at[1],
            device_id=device, device_id_type=MESH,
        ).start()

    for at in plane:
        to_device(near_sum, in_plane_at, near_sem, in_plane(*at))

    fields = jnp.concatenate([residue, first, jnp.zeros((128 - 2 * COLS, LINES), F32)], axis=0)
    high = fields.astype(BF16)
    low = (fields - high.astype(F32)).astype(BF16)
    across = (((1,), (1,)), ((), ()))
    placed = lax.dot_general(spread_ref[...], high, across, preferred_element_type=F32)
    placed = placed + lax.dot_general(spread_ref[...], low, across, preferred_element_type=F32)
    lane = lane_iota(WIDE, 128)
    for row in range(DENSE):
        packed = jnp.zeros((WIDE, 128), F32)
        for i in range(PLACES):
            begin = 48 * i - 128 * row
            if begin < 128 and begin + 48 > 0:
                turned = placed[i * WIDE : (i + 1) * WIDE]
                if begin % 128:
                    turned = pltpu.roll(turned, begin % 128, 1)
                packed = jnp.where((lane >= begin) & (lane < begin + 48), turned, packed)
        send_fields[:, row, :] = packed

    @pl.loop(0, WIDE // 2, unroll=8)
    def _(k):
        to_wide(far_first(k), lambda to: send_fields.at[to], got_fields.at[me], field_sem)

    finish(near_sum, near_sum, near_sem, PLANE - 1)
    far_sum[z_at] = jnp.sum(near_sum[...].reshape(PLANE, 128), axis=0, keepdims=True)
    for at in line:
        to_device(far_sum, z_at, far_sem, in_line(at))

    @pl.loop(WIDE // 2, WIDE - 1)
    def _(k):
        to_wide(far_first(k), lambda to: send_fields.at[to], got_fields.at[me], field_sem)

    def cross(rows, sems):
        @pl.loop(0, WIDE, unroll=8)
        def _(k):
            step = k // 8
            ahead_by = jnp.where(lax.rem(step, 2) == 1, (step + 1) // 2, 8 - step // 2)
            to = lax.rem(z_lo + ahead_by, 8) * 8 + lax.rem(me + 4 + k, 8)
            pltpu.make_async_remote_copy(
                src_ref=send_fields.at[to, pl.ds(0, rows)], dst_ref=got_cross.at[me, pl.ds(0, rows)],
                send_sem=sems.at[0], recv_sem=sems.at[1],
                device_id={"wide": to, "narrow": across_to}, device_id_type=MESH,
            ).start()

    @pl.when(crosses & (distance == 1))
    def _():
        cross(4, near_cross)

    @pl.when(crosses & (distance > 1))
    def _():
        cross(3, cross_sem)

    got_fields[me] = send_fields[me]

    finish(far_sum, far_sum, far_sem, LINE - 1)
    sums = jnp.sum(far_sum[...].reshape(LINE, 128), axis=0, keepdims=True)
    picked = [jnp.sum(jnp.where(lane1 == i, sums, 0.0), axis=1, keepdims=True) for i in range(4)]
    c0, c1 = step_scalars(*picked)
    solution_ref[...] = prior + c0 * residue + c1 * first

    finish(send_fields, got_fields, field_sem, WIDE - 1)
    def unpack(source):
        lines = [source[:, row, :] for row in range(DENSE)]
        pairs = []
        for m in range(6):
            begin = 96 * m
            row, off = begin // 128, begin % 128
            pair = pltpu.roll(lines[row], 128 - off, 1) if off else lines[row]
            if off + 96 > 128:
                pair = jnp.where(lane < 128 - off, pair, pltpu.roll(lines[row + 1], 128 - off, 1))
            pairs.append(pair)
        pairs = jnp.concatenate(pairs, axis=0)
        joined = c0 * pairs + c1 * pltpu.roll(pairs, 128 - COLS, 1)
        high = joined.astype(BF16)
        low = (joined - high.astype(F32)).astype(BF16)
        block_of = lax.broadcasted_iota(jnp.int32, (16, 2 * READOUT), 0)
        readout_of = lax.rem(lane_iota(16, 2 * READOUT), READOUT)
        inside = (readout_of >= COLS * block_of) & (readout_of < COLS * block_of + COLS)
        change = jnp.zeros((SLICES * 16, READOUT), F32)
        for part in (high, low):
            wide = dot(part, rep_ref[...]).reshape(6 * SLICES, 16, 2 * READOUT)
            wide = jnp.where(inside[None], wide, 0.0).reshape(6 * WIDE, 2 * READOUT).astype(BF16)
            wide = jnp.concatenate([wide[:, :READOUT], wide[:, READOUT:]], axis=0)
            change = change + dot(pick_ref[...], wide)
        return [change[16 * s : 16 * s + 16] for s in range(SLICES)]

    change = unpack(got_fields)
    cells = [cells[s] + change[s] for s in range(SLICES)]

    send_halo[0] = diamond(cells[3], cells[2], cells[1]).astype(BF16)
    send_halo[1] = diamond(cells[0], cells[1], cells[2]).astype(BF16)
    up, down = (
        pltpu.make_async_remote_copy(
            src_ref=send_halo.at[side], dst_ref=got_halo.at[side],
            send_sem=halo_send.at[side], recv_sem=halo_recv.at[side],
            device_id={"narrow": lax.rem(nme + step, NARROW)}, device_id_type=MESH,
        )
        for side, step in ((0, 1), (1, NARROW - 1))
    )

    @pl.when(x_at < 3)
    def _():
        up.start()

    @pl.when(x_at > 0)
    def _():
        down.start()

    def wait_cross(ref, count, rows, sem):
        part = ref.at[pl.ds(0, count), pl.ds(0, rows)]
        pltpu.make_async_copy(part, part, sem).wait()

    @pl.when(crosses & (distance == 1))
    def _():
        wait_cross(send_fields, WIDE, 4, near_cross.at[0])

    @pl.when(crosses & (distance > 1))
    def _():
        wait_cross(send_fields, WIDE, 3, cross_sem.at[0])

    @pl.when(middle_pair)
    def _():
        dia.wait()
        wait_cross(got_cross, 16, 4, near_cross.at[1])
        wait_cross(got_cross, 32, 3, cross_sem.at[1])

    crossed = unpack(got_cross)
    crossed = jnp.where(
        nme == 3, diamond(crossed[0], crossed[1], crossed[2]), diamond(crossed[3], crossed[2], crossed[1])
    )
    crossed = crossed + got_dia[...]

    @pl.when(x_at < 3)
    def _():
        up.wait_send()
        down.wait_recv()

    @pl.when(x_at > 0)
    def _():
        down.wait_send()
        up.wait_recv()

    def opened(rows):
        zero = jnp.zeros((8, READOUT), F32)
        near = jnp.concatenate([zero[:1], rows[:10], zero[:5]], axis=0)
        middle = jnp.concatenate([zero[:2], rows[10:18], zero[:6]], axis=0)
        far = jnp.concatenate([zero[:3], rows[18:24], zero[:7]], axis=0)
        return near, middle, far

    has_low = jnp.where(nme > 0, 1.0, 0.0).astype(F32)
    has_high = jnp.where(nme < NARROW - 1, 1.0, 0.0).astype(F32)
    near_low, mid_low, far_low = opened(jnp.where(nme == 4, crossed, got_halo[0].astype(F32)))
    near_high, mid_high, far_high = opened(jnp.where(nme == 3, crossed, got_halo[1].astype(F32)))
    volume = [far_low, mid_low, near_low] + cells + [near_high, mid_high, far_high]
    keeps = [has_low] * 3 + [None] * SLICES + [has_high] * 3
    margin = jnp.zeros((16, 128), F32)
    volume = [jnp.concatenate([one, margin], axis=1) for one in volume]
    line_of = lax.broadcasted_iota(jnp.int32, (16, READOUT + 128), 0) + (ROWS * me - EDGE)
    in_grid = (line_of >= 0) & (line_of < LINES) & (lane_iota(16, READOUT + 128) < READOUT)
    in_grid = in_grid.astype(F32)

    def flux(jump):
        return jump / (1.0 + jump * jump)

    for step in range(DIFF_STEPS):
        last = len(volume) - 1
        across_slices = [flux(volume[i + 1] - volume[i]) for i in range(last)]
        after = []
        for i in range(1, last):
            one = volume[i]
            down = flux(pltpu.roll(one, 15, 0) - one)
            along = flux(pltpu.roll(one, SPAN - 1, 1) - one)
            moved = axis_weights[0] * (down - pltpu.roll(down, 1, 0))
            moved = moved + axis_weights[1] * (across_slices[i] - across_slices[i - 1])
            moved = moved + axis_weights[2] * (along - pltpu.roll(along, 1, 1))
            grid = in_grid if keeps[i] is None else in_grid * keeps[i]
            after.append((one + time_step * moved) * grid)
        volume = after
        keeps = keeps[1:-1]
    for s in range(SLICES):
        for i in range(ROWS):
            denoised_ref[i, s : s + 1, :] = volume[s][EDGE + i : EDGE + i + 1, :READOUT]


def whole(prior, coil_maps, kspace, band_start, frac, mask):
    vmem = pl.BlockSpec(memory_space=pltpu.VMEM)
    far = pl.BlockSpec(memory_space=pltpu.HBM)
    table = cosine_table()
    constants = (table, table.T) + place_tables() + return_tables()
    constants = [jnp.asarray(one, BF16) for one in constants]
    moved = [kspace, frac] + constants + [prior, coil_maps, band_start]
    return pl.pallas_call(
        whole_body,
        out_shape=(
            jax.ShapeDtypeStruct((COLS, LINES), F32),
            jax.ShapeDtypeStruct((ROWS, SLICES, READOUT), F32),
        ),
        in_specs=[far] * (len(moved) + 1),
        out_specs=(vmem, vmem),
        scratch_shapes=[pltpu.SMEM(mask.shape, mask.dtype)]
        + [pltpu.VMEM(one.shape, one.dtype) for one in moved]
        + [
            pltpu.VMEM((WIDE, 8, LINES), BF16),
            pltpu.VMEM((WIDE, 8, LINES), BF16),
            pltpu.VMEM((2, EDGE, SLICES, READOUT), F32),
            pltpu.VMEM((COLS, COILS, LINES), F32),
            pltpu.VMEM((TAPS, 2 * COLS, LINES), F32),
            pltpu.VMEM((2, COLS * COILS, LINES), F32),
            pltpu.VMEM((2 * COLS, SPAN), jnp.int32),
            pltpu.VMEM((WIDE, DENSE, 128), F32),
            pltpu.VMEM((WIDE, DENSE, 128), F32),
            pltpu.VMEM((PLANE, 1, 128), F32),
            pltpu.VMEM((LINE, 1, 128), F32),
            pltpu.VMEM((2, HALO, READOUT), BF16),
            pltpu.VMEM((2, HALO, READOUT), BF16),
            pltpu.VMEM((WIDE, DENSE, 128), F32),
            pltpu.VMEM((HALO, READOUT), F32),
            pltpu.VMEM((HALO, READOUT), F32),
            pltpu.SemaphoreType.DMA((len(moved) + 1,)),
            pltpu.SemaphoreType.DMA((2,)),
            pltpu.SemaphoreType.DMA((2,)),
            pltpu.SemaphoreType.DMA((2,)),
            pltpu.SemaphoreType.DMA((2,)),
            pltpu.SemaphoreType.DMA((2,)),
            pltpu.SemaphoreType.DMA((2,)),
            pltpu.SemaphoreType.DMA((2,)),
            pltpu.SemaphoreType.DMA((2,)),
            pltpu.SemaphoreType.DMA((2,)),
            pltpu.SemaphoreType.DMA((2,)),
            pltpu.SemaphoreType.DMA((2,)),
        ],
        compiler_params=pltpu.CompilerParams(collective_id=0, has_side_effects=True, vmem_limit_bytes=63 << 20),
        name="whole",
    )(mask, *moved)


def per_device(prior, coil_maps, kspace, band_start, band_frac, shot_mask):
    solved, denoised = whole(
        prior, coil_maps, kspace, band_start, jnp.transpose(band_frac, (0, 2, 1)), jnp.transpose(shot_mask, (0, 2, 1))
    )
    return jnp.transpose(solved), denoised


def solution(mesh):
    in_specs = (
        P("wide", "narrow", None),
        P("wide", "narrow"),
        P(None, None, ("narrow", "wide")),
        P(None, ("narrow", "wide")),
        P(None, None, ("narrow", "wide")),
        P(None, None, "narrow"),
    )
    out_specs = (P(None, ("narrow", "wide")), P("wide", "narrow", None))
    return jax.shard_map(per_device, mesh=mesh, in_specs=in_specs, out_specs=out_specs, check_vma=False)
```
